128 devices in a mesh: mesh: 32 (over x, z, core), grp: 4 (over y).
Axes of the slice: x: 4, y: 4, z: 4, core: 2. Of those that a mesh axis runs over, the one named last changes fastest.
Arguments:
- forcing: float32 [32, 524288], P(None, ('mesh', 'grp')), may hold values from -134 to 134
- plan: int32 [128, 64], P(('mesh', 'grp')), may hold values from 0 to 63, each once within a row
- lower_blocks: float32 [256, 458752], P(None, ('mesh', 'grp')), may hold values from -0.25 to 0.25
- lower_columns: int32 [7168, 4], P(('mesh', 'grp')), may hold values from 0 to 15
- upper_blocks: float32 [256, 458752], P(None, ('mesh', 'grp')), may hold values from -0.25 to 0.25
- upper_columns: int32 [7168, 4], P(('mesh', 'grp')), may hold values from 0 to 15
- diag_blocks: float32 [64, 524288], P(None, ('mesh', 'grp')), may hold values from -0.5 to 4.5
- inverse_blocks: float32 [64, 524288], P(None, ('mesh', 'grp')), may hold values from -0.1 to 0.75
- halo_list: int32 [1024, 4], P(('mesh', 'grp')), may hold values from 0 to 7
Outputs:
- basis: float32 [32, 524288], P(None, ('mesh', 'grp'))
- adjoint_field: float32 [32, 524288], P(None, ('mesh', 'grp'))
The draws below stay inside these ranges and needn't reach their ends.
Inputs may be any that keep to these rules, and one draw needn't show every extreme that they name: Each row of plan is a permutation of 0 to 63.
All inputs are finite; a program needn't handle non-finite values.
Results may differ from the reference program's by a relative error of at most 0.00011.
Values sent between devices are 32-bit elements; how exact they have to be, the bound alone decides.
No kernel may reach another device: no remote copies, remote signals or barrier semaphores. Data moves between devices by JAX's collectives and lax.ppermute only.
A program may use at most 128 MiB of HBM per device.

```python
import math
import jax
import jax.numpy as jnp
from jax import lax

S = 32
BLOCK = 64
KL = 4
KU = 4
LEV = 8
RPL = 8
HB = 4
NB = 64
SHARDS = 128
NBLK = 8192
NROWS = 524288


def diagonal_scale(key, power):
    level = jax.random.uniform(key, (NBLK * BLOCK,), minval=0.0, maxval=1.0)
    return 1.5 * jnp.exp(math.log(4.0 / 1.5) * level ** power)


def identity_mask():
    return (jnp.arange(BLOCK)[:, None] == jnp.arange(NBLK * BLOCK)[None, :] % BLOCK).astype(jnp.float32)


def draw_forcing(key, part):
    key = jax.random.fold_in(key, 5)
    keys = jax.random.split(key, 3)
    row_scale = jnp.exp(jax.random.uniform(keys[0], (1, NROWS), minval=0.0, maxval=math.log(10.0)))
    column_scale = jnp.exp(jax.random.uniform(keys[1], (S, 1), minval=0.0, maxval=math.log(10.0)))
    base = jnp.clip(jax.random.normal(keys[2], (S, NROWS)), -4.0, 4.0)
    return (base * row_scale * column_scale / 3.0).astype(jnp.float32)


def draw_diag_blocks(key, part):
    power = 1.0
    scale = diagonal_scale(key, power)
    key = jax.random.fold_in(key, 21)
    noise = jnp.clip(jax.random.normal(key, (BLOCK, NBLK * BLOCK)), -4.0, 4.0)
    values = scale[None, :] * (identity_mask() + 0.03 * noise)
    return values.astype(jnp.float32)


def draw_inverse_blocks(key, part):
    power = 1.0
    scale = diagonal_scale(key, power)
    key = jax.random.fold_in(key, 37)
    noise = jnp.clip(jax.random.normal(key, (BLOCK, NBLK * BLOCK)), -4.0, 4.0)
    values = (identity_mask() + 0.03 * noise) / scale[None, :]
    return values.astype(jnp.float32)


def touch_ends(values, rng, smallest, top_value):
    extent = values.shape
    index_at = [jax.random.randint(jax.random.fold_in(rng, axis), (), 0, extent[axis]) for axis in range(len(extent))]
    values = values.at[tuple(index_at)].set(smallest)
    longest = extent.index(max(extent))
    index_at[longest] = (index_at[longest] + 1) % extent[longest]
    return values.at[tuple(index_at)].set(top_value)


def steps_of(stream_key, shape, cuts, smallest, top_value):
    def one(dim, blocks):
        steps = jax.random.uniform(jax.random.fold_in(jax.random.fold_in(stream_key, 6), dim), (blocks,), jnp.float32, smallest / len(cuts), top_value / len(cuts))
        return jnp.repeat(jnp.exp(steps), shape[dim] // blocks).reshape((-1,) + (1,) * (len(shape) - dim - 1))

    loudness = one(*cuts[0])
    for cut in cuts[1:]:
        loudness = loudness * one(*cut)
    return loudness


def centred(own_key, extent, deviation, most, cuts=(), dtype=jnp.bfloat16):
    level = steps_of(own_key, extent, cuts, -0.22, 0.18) if cuts else 1.0
    values = jax.random.normal(own_key, extent, jnp.float32) * deviation * level
    return jnp.minimum(jnp.maximum(values, -most), most).astype(dtype)


def setup_inputs(seed: int = 0) -> dict:
    streams_of = jax.random.split(jax.random.key(seed), 10)
    forcing = draw_forcing(jax.random.fold_in(streams_of[9], 71), 0)
    plan = jax.vmap(lambda own: jax.random.permutation(own, NB))(jax.random.split(streams_of[1], SHARDS)).reshape((SHARDS, NB)).astype(jnp.int32)
    lower_blocks = centred(streams_of[2], (KL * BLOCK, SHARDS * (LEV - 1) * RPL * BLOCK), (2 * KL * BLOCK) ** -0.5, 0.25, ((1, 128),), jnp.float32)
    lower_columns = touch_ends(jax.random.randint(streams_of[3], (SHARDS * (LEV - 1) * RPL, KL), 0, RPL + 2 * HB), jax.random.fold_in(streams_of[3], 1), 0, (RPL + 2 * HB) - 1).astype(jnp.int32)
    upper_blocks = centred(streams_of[4], (KU * BLOCK, SHARDS * (LEV - 1) * RPL * BLOCK), (2 * KU * BLOCK) ** -0.5, 0.25, ((1, 128),), jnp.float32)
    upper_columns = touch_ends(jax.random.randint(streams_of[5], (SHARDS * (LEV - 1) * RPL, KU), 0, RPL + 2 * HB), jax.random.fold_in(streams_of[5], 1), 0, (RPL + 2 * HB) - 1).astype(jnp.int32)
    diag_blocks = draw_diag_blocks(jax.random.fold_in(streams_of[9], 71), 0)
    inverse_blocks = draw_inverse_blocks(jax.random.fold_in(streams_of[9], 71), 0)
    halo_list = touch_ends(jax.random.randint(streams_of[8], (SHARDS * LEV, HB), 0, RPL), jax.random.fold_in(streams_of[8], 1), 0, RPL - 1).astype(jnp.int32)
    return dict(forcing=forcing, plan=plan, lower_blocks=lower_blocks, lower_columns=lower_columns, upper_blocks=upper_blocks, upper_columns=upper_columns, diag_blocks=diag_blocks, inverse_blocks=inverse_blocks, halo_list=halo_list)


HIGH = lax.Precision.HIGHEST

def toward_higher(values):
    return jnp.concatenate([jnp.zeros_like(values[:, :1]), values[:, :-1]], axis=1)

def toward_lower(values):
    return jnp.concatenate([values[:, 1:], jnp.zeros_like(values[:, :1])], axis=1)

def slot_values(source, rows):
    shards = jnp.arange(source.shape[1])[:, None]
    chosen = source[:, shards, rows]
    return jnp.concatenate([source, toward_higher(chosen), toward_lower(chosen)], axis=2)

def block_product(slots, columns, blocks):
    shards = jnp.arange(slots.shape[1])[:, None, None]
    picked = slots[:, shards, columns]
    picked = picked.reshape(picked.shape[0], picked.shape[1], picked.shape[2], -1)
    return jnp.einsum('sdjq,qdjr->sdjr', picked, blocks, precision=HIGH)

def diagonal_product(blocks, values):
    return jnp.einsum('sdjc,cdjr->sdjr', values, blocks, precision=HIGH)

def diagonal_transposed(blocks, values):
    return jnp.einsum('sdjr,cdjr->sdjc', values, blocks, precision=HIGH)

def push_terms(values, columns, blocks, rows):
    terms = jnp.einsum('sdjr,qdjr->sdjq', values, blocks, precision=HIGH)
    terms = terms.reshape(terms.shape[0], terms.shape[1], terms.shape[2], columns.shape[-1], BLOCK)
    shards = jnp.arange(values.shape[1])[:, None, None]
    slots = jnp.zeros((values.shape[0], values.shape[1], RPL + 2 * HB, BLOCK), jnp.float32)
    slots = slots.at[:, shards, columns].add(terms)
    arriving = toward_lower(slots[:, :, RPL:RPL + HB]) + toward_higher(slots[:, :, RPL + HB:])
    owners = jnp.arange(values.shape[1])[:, None]
    return slots[:, :, :RPL].at[:, owners, rows].add(arriving)

def precondition(right, lower, lower_columns, upper, upper_columns, inverse, halo):
    forward = []
    for level in range(LEV):
        term = right[level]
        if level > 0:
            slots = slot_values(forward[level - 1], halo[:, level - 1])
            term = term - block_product(slots, lower_columns[:, level - 1], lower[:, :, level - 1])
        forward.append(diagonal_product(inverse[:, :, level], term))
    result = [None] * LEV
    result[LEV - 1] = forward[LEV - 1]
    for level in range(LEV - 2, -1, -1):
        slots = slot_values(result[level + 1], halo[:, level + 1])
        term = block_product(slots, upper_columns[:, level], upper[:, :, level])
        result[level] = forward[level] - diagonal_product(inverse[:, :, level], term)
    return result

def operate(field, diagonal, lower, lower_columns, upper, upper_columns, halo):
    image = []
    for level in range(LEV):
        term = diagonal_product(diagonal[:, :, level], field[level])
        if level > 0:
            slots = slot_values(field[level - 1], halo[:, level - 1])
            term = term + block_product(slots, lower_columns[:, level - 1], lower[:, :, level - 1])
        if level < LEV - 1:
            slots = slot_values(field[level + 1], halo[:, level + 1])
            term = term + block_product(slots, upper_columns[:, level], upper[:, :, level])
        image.append(term)
    return image

def adjoint(source, lower, lower_columns, upper, upper_columns, inverse, halo):
    before = [None] * LEV
    after = [None] * LEV
    before[0] = source[0]
    after[0] = diagonal_transposed(inverse[:, :, 0], before[0])
    for level in range(LEV - 1):
        incoming = push_terms(after[level], upper_columns[:, level], upper[:, :, level], halo[:, level + 1])
        before[level + 1] = source[level + 1] - incoming
        after[level + 1] = diagonal_transposed(inverse[:, :, level + 1], before[level + 1])
    result = [None] * LEV
    result[LEV - 1] = diagonal_transposed(inverse[:, :, LEV - 1], before[LEV - 1])
    for level in range(LEV - 2, -1, -1):
        incoming = push_terms(result[level + 1], lower_columns[:, level], lower[:, :, level], halo[:, level])
        result[level] = diagonal_transposed(inverse[:, :, level], before[level] - incoming)
    return result

def into_levels(matrix, order):
    shards = jnp.arange(SHARDS)[:, None]
    blocks = matrix.reshape(matrix.shape[0], SHARDS, NB, BLOCK)[:, shards, order]
    blocks = blocks.reshape(matrix.shape[0], SHARDS, LEV, RPL, BLOCK)
    return [blocks[:, :, level] for level in range(LEV)]

def out_of_levels(levels, order):
    shards = jnp.arange(SHARDS)[:, None]
    stacked = jnp.stack(levels, axis=2).reshape(levels[0].shape[0], SHARDS, NB, BLOCK)
    natural = jnp.zeros_like(stacked).at[:, shards, order].set(stacked)
    return natural.reshape(levels[0].shape[0], -1)

def orthonormal(sketch):
    for repeat in range(2):
        gram = jnp.dot(sketch, sketch.T, precision=HIGH)
        factor = jnp.linalg.cholesky(gram)
        sketch = jax.scipy.linalg.solve_triangular(factor, sketch, lower=True)
    return sketch

def reference(forcing, plan, lower_blocks, lower_columns, upper_blocks, upper_columns, diag_blocks, inverse_blocks, halo_list):
    lower = lower_blocks.reshape(KL * BLOCK, SHARDS, LEV - 1, RPL, BLOCK)
    upper = upper_blocks.reshape(KU * BLOCK, SHARDS, LEV - 1, RPL, BLOCK)
    lower_index = lower_columns.reshape(SHARDS, LEV - 1, RPL, KL)
    upper_index = upper_columns.reshape(SHARDS, LEV - 1, RPL, KU)
    diagonal = diag_blocks.reshape(BLOCK, SHARDS, LEV, RPL, BLOCK)
    inverse = inverse_blocks.reshape(BLOCK, SHARDS, LEV, RPL, BLOCK)
    halo = halo_list.reshape(SHARDS, LEV, HB)
    right = into_levels(forcing, plan)
    first = precondition(right, lower, lower_index, upper, upper_index, inverse, halo)
    image = operate(first, diagonal, lower, lower_index, upper, upper_index, halo)
    residual = [right[level] - image[level] for level in range(LEV)]
    second = precondition(residual, lower, lower_index, upper, upper_index, inverse, halo)
    sketch = out_of_levels([first[level] + second[level] for level in range(LEV)], plan)
    basis = math.sqrt(NROWS) * orthonormal(sketch)
    result = adjoint(into_levels(basis, plan), lower, lower_index, upper, upper_index, inverse, halo)
    return (basis, out_of_levels(result, plan))
```

```python
import functools
import math

import jax
import jax.numpy as jnp
from jax import lax
from jax.experimental import pallas as pl
from jax.experimental.pallas import tpu as pltpu
from jax.sharding import PartitionSpec as P

S = 32
BLOCK = 64
KL = 4
LEV = 8
RPL = 8
HB = 4
NB = 64
PAIR = 2 * BLOCK
QUAD = 4 * BLOCK
WIDE = RPL * BLOCK

LOWER_AT = 0
UPPER_AT = (LEV - 1) * RPL * KL
HALO_AT = 2 * UPPER_AT
PLAN_AT = HALO_AT + LEV * HB
PARITY_AT = PLAN_AT + NB

HIGH = lax.Precision.HIGHEST
AXES = ("mesh", "grp")
VMEM = pltpu.CompilerParams(vmem_limit_bytes=40 * 1024 * 1024)


def split(x):
    high = x.astype(jnp.bfloat16)
    low = (x - high.astype(jnp.float32)).astype(jnp.bfloat16)
    return high, low


def dot(a, b, dims=((1,), (0,))):
    return lax.dot_general(a, b, (dims, ((), ())), preferred_element_type=jnp.float32)


def dot3(a, b_high, b_low, dims=((1,), (0,))):
    a_high, a_low = split(a)
    return dot(a_high, b_high, dims) + (dot(a_low, b_high, dims) + dot(a_high, b_low, dims))


def first_half():
    return lax.broadcasted_iota(jnp.int32, (S, PAIR), 1) < BLOCK


def turned(tile):
    return pltpu.roll(tile, BLOCK, 1)


def doubled(tile):
    first = first_half()
    other = turned(tile)
    return jnp.where(first, tile, other), jnp.where(first, other, tile)


def parity_of(index):
    return jnp.bitwise_and(index, 1)


def pair_tile(ref, block):
    start = pl.multiple_of(lax.shift_right_logical(block, 1) * PAIR, PAIR)
    return pl.ds(start, PAIR)


def in_half(tile, block, half):
    return jnp.where(parity_of(block) == half, tile, turned(tile))


def listed(ints, level, ref):
    tiles = []
    first = first_half()
    for pair in range(HB // 2):
        h = [ints[HALO_AT + level * HB + 2 * pair + half] for half in range(2)]
        moved = [in_half(ref[:, pair_tile(ref, h[half])], h[half], half) for half in range(2)]
        tiles.append(jnp.where(first, moved[0], moved[1]))
    return jnp.concatenate(tiles, axis=1)


def own_blocks(out):
    first = first_half()
    rows = [out[j * S : (j + 1) * S] for j in range(4)]
    return jnp.concatenate(
        [
            jnp.where(first, rows[0][:, :PAIR], rows[1][:, :PAIR]),
            jnp.where(first, rows[2][:, PAIR:], rows[3][:, PAIR:]),
        ],
        axis=1,
    )


def spread(quad):
    lane = lax.shift_right_logical(lax.broadcasted_iota(jnp.int32, (S, QUAD), 1), 6)
    return jnp.concatenate([jnp.where(lane == j, quad, 0.0) for j in range(4)], axis=0)


def stacked(quad):
    parts = []
    for pair in range(2):
        tile = quad[:, pair * PAIR : (pair + 1) * PAIR]
        parts += [tile[:, :BLOCK], turned(tile)[:, :BLOCK]]
    return jnp.concatenate(parts, axis=0)


def send_listed_kernel(level, ints, field, send):
    send[...] = listed(ints, level, field)


def prepare_kernel(ints, forcing, inverse, y, send):
    for quad in range(NB // 4):
        rows = []
        for j in range(4):
            block = ints[PLAN_AT + 4 * quad + j]
            tile = forcing[:, pair_tile(forcing, block)]
            rows.append(in_half(tile, block, 0)[:, :BLOCK])
        lanes = slice(quad * QUAD, (quad + 1) * QUAD)
        inv_high, inv_low = split(inverse[:, lanes])
        y[:, lanes] = own_blocks(dot3(jnp.concatenate(rows, axis=0), inv_high, inv_low))
    send[...] = listed(ints, 0, y)


def compose_kernel(blocks, inverse, high, low):
    lane = lax.shift_right_logical(lax.broadcasted_iota(jnp.int32, (BLOCK, QUAD), 1), 6)
    for quad in range(2):
        lanes = slice(quad * QUAD, (quad + 1) * QUAD)
        inv = inverse[:, lanes]
        diagonal = jnp.concatenate([jnp.where(lane == j, inv, 0.0) for j in range(4)], axis=0)
        d_high, d_low = split(diagonal)
        product = dot3(blocks[:, lanes], d_high, d_low)
        p_high, p_low = split(product)
        high[:, lanes] = p_high
        low[:, lanes] = p_low


def combine_kernel(ints, x, y, w, diag, inverse, out):
    for quad in range(x.shape[1] // QUAD):
        lanes = slice(quad * QUAD, (quad + 1) * QUAD)
        d_high, d_low = split(diag[:, lanes])
        i_high, i_low = split(inverse[:, lanes])
        value = x[:, lanes]
        image = own_blocks(dot3(stacked(value), d_high, d_low))
        image = own_blocks(dot3(stacked(image), i_high, i_low))
        out[:, lanes] = 2.0 * value + y[:, lanes] - w[:, lanes] - image


def fill_slots(ints, slots, prev, swap0, swap1):
    for pair in range(RPL // 2):
        a, b = doubled(prev[:, pair * PAIR : (pair + 1) * PAIR])
        slots[2 * pair] = a
        slots[2 * pair + 1] = b
    odd = ints[PARITY_AT]
    for ref, base in ((swap1, RPL + HB * odd), (swap0, RPL + HB - HB * odd)):
        for pair in range(HB // 2):
            a, b = doubled(ref[:, pair * PAIR : (pair + 1) * PAIR])
            slots[base + 2 * pair] = a
            slots[base + 2 * pair + 1] = b


def gather_kernel(at, level, send_on, ints, base, high, low, prev, swap0, swap1, out, *rest):
    slots = rest[-1]
    fill_slots(ints, slots, prev, swap0, swap1)
    first = first_half()
    for quad in range(2):
        rows = []
        for j in range(4):
            c = [ints[at + (quad * 4 + j) * KL + k] for k in range(KL)]
            rows.append(
                jnp.concatenate(
                    [
                        jnp.where(first, slots[c[0]], slots[c[1]]),
                        jnp.where(first, slots[c[2]], slots[c[3]]),
                    ],
                    axis=1,
                )
            )
        lanes = slice(quad * QUAD, (quad + 1) * QUAD)
        product = dot3(jnp.concatenate(rows, axis=0), high[:, lanes], low[:, lanes])
        out[:, lanes] = base[:, lanes] - own_blocks(product)
    if send_on:
        rest[0][...] = listed(ints, level, out)


def add_listed(ints, level, out, arriving):
    first = first_half()
    for i in range(HB):
        h = ints[HALO_AT + level * HB + i]
        tile = arriving[:, (i // 2) * PAIR : (i // 2 + 1) * PAIR]
        tile = jnp.where(parity_of(h) == i % 2, tile, turned(tile))
        keep = first == (parity_of(h) == 0)
        lanes = pair_tile(out, h)
        out[:, lanes] = out[:, lanes] - jnp.where(keep, tile, 0.0)


def push_kernel(at, level, first_level, last_level, ints, *refs):
    refs = list(refs)
    source = refs.pop(0)
    if not first_level:
        own_in, swap0, swap1 = refs.pop(0), refs.pop(0), refs.pop(0)
    if not last_level:
        high, low = refs.pop(0), refs.pop(0)
    if not first_level:
        out = refs.pop(0)
        out[...] = source[...] - own_in[...]
        add_listed(ints, level, out, swap0[...] + swap1[...])
    else:
        out = source
    if last_level:
        return
    own, send0, send1, slots = refs
    slots[...] = jnp.zeros_like(slots)
    first = first_half()
    for quad in range(2):
        lanes = slice(quad * QUAD, (quad + 1) * QUAD)
        terms = dot3(spread(out[:, lanes]), high[:, lanes], low[:, lanes], ((1,), (1,)))
        for j in range(4):
            for k in range(KL):
                c = ints[at + (quad * 4 + j) * KL + k]
                tile = terms[j * S : (j + 1) * S, (k // 2) * PAIR : (k // 2 + 1) * PAIR]
                keep = first if k % 2 == 0 else jnp.logical_not(first)
                slots[c] += jnp.where(keep, tile, 0.0)

    def total(c):
        value = slots[c]
        return value + turned(value)

    for pair in range(RPL // 2):
        own[:, pair * PAIR : (pair + 1) * PAIR] = jnp.where(
            first, total(2 * pair), total(2 * pair + 1)
        )
    odd = ints[PARITY_AT]
    for ref, base in ((send1, RPL + HB * odd), (send0, RPL + HB - HB * odd)):
        for pair in range(HB // 2):
            ref[:, pair * PAIR : (pair + 1) * PAIR] = jnp.where(
                first, total(base + 2 * pair), total(base + 2 * pair + 1)
            )


def finish_kernel(ints, turn, field, inverse, out, natural):
    first = first_half()
    for quad in range(NB // 4):
        lanes = slice(quad * QUAD, (quad + 1) * QUAD)
        i_high, i_low = split(inverse[:, lanes])
        product = dot3(spread(field[:, lanes]), i_high, i_low, ((1,), (1,)))
        for j in range(4):
            block = ints[PLAN_AT + 4 * quad + j]
            piece = product[j * S : (j + 1) * S]
            piece = jnp.concatenate([piece, piece], axis=1)
            place(natural, block, piece, first)
    out[...] = lax.dot_general(
        turn[...], natural[...], (((1,), (0,)), ((), ())), precision=HIGH, preferred_element_type=jnp.float32
    )


def place(natural, block, piece, first):
    keep = first == (parity_of(block) == 0)
    lanes = pair_tile(natural, block)
    natural[:, lanes] = jnp.where(keep, piece, natural[:, lanes])


def basis_kernel(ints, turn, field, out, natural):
    first = first_half()
    for pair in range(NB // 2):
        a, b = doubled(field[:, pair * PAIR : (pair + 1) * PAIR])
        place(natural, ints[PLAN_AT + 2 * pair], a, first)
        place(natural, ints[PLAN_AT + 2 * pair + 1], b, first)
    out[...] = lax.dot_general(
        turn[...], natural[...], (((1,), (0,)), ((), ())), precision=HIGH, preferred_element_type=jnp.float32
    )


SMEM_SPEC = pl.BlockSpec(memory_space=pltpu.SMEM)
VMEM_SPEC = pl.BlockSpec(memory_space=pltpu.VMEM)


def call(kernel, operands, outs, scratch=(), flops=0, smem=True):
    in_specs = [VMEM_SPEC] * len(operands)
    if smem:
        in_specs[0] = SMEM_SPEC
    moved = 4 * sum(math.prod(o.shape) for o in operands) + 4 * sum(math.prod(o) for o, _ in outs)
    return pl.pallas_call(
        kernel,
        out_shape=[jax.ShapeDtypeStruct(shape, dtype) for shape, dtype in outs],
        in_specs=in_specs,
        out_specs=[VMEM_SPEC] * len(outs),
        scratch_shapes=list(scratch),
        compiler_params=VMEM,
        cost_estimate=pl.CostEstimate(flops=flops, bytes_accessed=moved, transcendentals=0),
    )(*operands)


F32 = jnp.float32
BF16 = jnp.bfloat16
LEVEL_FIELD = ((S, WIDE), F32)
SENT = ((S, HB * BLOCK), F32)
SLOTS = pltpu.VMEM((RPL + 2 * HB, S, PAIR), F32)


def swap(sent0, sent1):
    count = lax.axis_size(AXES)
    even = [(i, i ^ 1) for i in range(count)]
    other = [((i + 1) ^ 1) - 1 for i in range(count)]
    odd = [(i, j) for i, j in enumerate(other) if 0 <= j < count]
    swap1 = lax.ppermute(sent1, AXES, odd)
    swap0 = lax.ppermute(sent0, AXES, even)
    return swap0, swap1


def shards(forcing, plan, lower_blocks, lower_columns, upper_blocks, upper_columns, diag_blocks, inverse_blocks, halo_list):
    parity = lax.rem(lax.axis_index(AXES), 2).astype(jnp.int32)
    ints = jnp.concatenate(
        [
            lower_columns.reshape(-1),
            upper_columns.reshape(-1),
            halo_list.reshape(-1),
            plan.reshape(-1),
            parity.reshape(1),
        ]
    )

    def level_of(array, level):
        return array[:, level * WIDE : (level + 1) * WIDE]

    y, sent = call(prepare_kernel, [ints, forcing, inverse_blocks], [((S, NB * BLOCK), F32), SENT])
    lower = []
    upper = []
    wide = ((KL * BLOCK, WIDE), BF16)
    for level in range(LEV - 1):
        lower.append(
            call(
                compose_kernel,
                [level_of(lower_blocks, level), level_of(inverse_blocks, level + 1)],
                [wide, wide],
                flops=2 * 6 * 256**3,
                smem=False,
            )
        )
    for level in range(LEV - 1):
        upper.append(
            call(
                compose_kernel,
                [level_of(upper_blocks, level), level_of(inverse_blocks, level)],
                [wide, wide],
                flops=2 * 6 * 256**3,
                smem=False,
            )
        )

    def gather(base, blocks, at, level, prev, sent, send_on):
        swap0, swap1 = swap(sent, sent)
        outs = call(
            functools.partial(gather_kernel, at, level, send_on),
            [ints, base, *blocks, prev, swap0, swap1],
            [LEVEL_FIELD, SENT] if send_on else [LEVEL_FIELD],
            [SLOTS],
        )
        return (outs[0], outs[1]) if send_on else (outs[0], None)

    def ascend(base, sent):
        field = [base[0]]
        for level in range(1, LEV):
            value, sent = gather(
                base[level], lower[level - 1], LOWER_AT + (level - 1) * RPL * KL, level, field[-1], sent, True
            )
            field.append(value)
        return field, sent

    def descend(base, sent):
        field = [None] * LEV
        field[LEV - 1] = base[LEV - 1]
        for level in range(LEV - 2, -1, -1):
            field[level], sent = gather(
                base[level], upper[level], UPPER_AT + level * RPL * KL, level, field[level + 1], sent, level > 0
            )
        return field

    y = [level_of(y, level) for level in range(LEV)]
    w, sent = ascend(y, sent)
    x = descend(w, sent)

    def combine(levels):
        join = lambda field: jnp.concatenate([field[level] for level in levels], axis=1) if len(levels) > 1 else field[levels[0]]
        part = slice(levels[0] * WIDE, (levels[-1] + 1) * WIDE)
        out = call(
            combine_kernel,
            [ints, join(x), join(y), join(w), diag_blocks[:, part], inverse_blocks[:, part]],
            [((S, WIDE * len(levels)), F32)],
        )[0]
        return [out[:, i * WIDE : (i + 1) * WIDE] for i in range(len(levels))]

    c = combine([0])
    sent = call(functools.partial(send_listed_kernel, 0), [ints, c[0]], [SENT])[0]
    for level in range(1, LEV):
        c += combine([level])
    v, sent = ascend(c, sent)
    sketch = descend([v[level] + w[level] - x[level] for level in range(LEV)], sent)

    def push(source, level, own, swaps, blocks, at):
        outs = [] if own is None else [LEVEL_FIELD]
        operands = [ints, source] + ([] if own is None else [own, *swaps])
        if blocks is not None:
            operands += blocks
            outs = outs + [LEVEL_FIELD, SENT, SENT]
        results = list(
            call(
                functools.partial(push_kernel, at, level, own is None, blocks is None),
                operands,
                outs,
                [SLOTS] if blocks is not None else [],
            )
        )
        value = source if own is None else results.pop(0)
        if blocks is None:
            return value, None, None
        return value, results[0], swap(results[1], results[2])

    before = [None] * LEV
    own = swaps = None
    for level in range(LEV - 1):
        before[level], own, swaps = push(sketch[level], level, own, swaps, upper[level], UPPER_AT + level * RPL * KL)
    last = LEV - 1
    turned_back = [None] * LEV
    before[last], _, _ = push(sketch[last], last, own, swaps, None, 0)
    own = swaps = None
    for level in range(LEV - 1, 0, -1):
        turned_back[level], own, swaps = push(
            before[level], level, own, swaps, lower[level - 1], LOWER_AT + (level - 1) * RPL * KL
        )
    turned_back[0], _, _ = push(before[0], 0, own, swaps, None, 0)

    columns = jnp.concatenate(sketch, axis=1)
    gram = lax.psum(jnp.dot(columns, columns.T, precision=HIGH), AXES)
    unit = jnp.eye(S, dtype=F32)
    first = jax.scipy.linalg.solve_triangular(jnp.linalg.cholesky(gram), unit, lower=True)
    ortho = jnp.dot(first, columns, precision=HIGH)
    gram = lax.psum(jnp.dot(ortho, ortho.T, precision=HIGH), AXES)
    second = jax.scipy.linalg.solve_triangular(jnp.linalg.cholesky(gram), unit, lower=True)
    second = second * math.sqrt(NB * BLOCK * lax.axis_size(AXES))
    both = jnp.dot(second, first, precision=HIGH)
    natural = [((S, NB * BLOCK), F32)]
    room = [pltpu.VMEM((S, NB * BLOCK), F32)]
    basis = call(basis_kernel, [ints, second, ortho], natural, room)[0]
    field = jnp.concatenate(turned_back, axis=1)
    adjoint_field = call(finish_kernel, [ints, both, field, inverse_blocks], natural, room)[0]
    return (basis, adjoint_field)


def solution(mesh):
    in_specs = (
        P(None, AXES),
        P(AXES, None),
        P(None, AXES),
        P(AXES, None),
        P(None, AXES),
        P(AXES, None),
        P(None, AXES),
        P(None, AXES),
        P(AXES, None),
    )
    out_specs = (P(None, AXES), P(None, AXES))
    return jax.shard_map(shards, mesh=mesh, in_specs=in_specs, out_specs=out_specs, check_vma=False)
```

```python
import functools
import math

import jax
import jax.numpy as jnp
from jax import lax
from jax.experimental import pallas as pl
from jax.experimental.pallas import tpu as pltpu
from jax.sharding import PartitionSpec as P

S = 32
BLOCK = 64
KL = 4
LEV = 8
RPL = 8
HB = 4
NB = 64
PAIR = 2 * BLOCK
QUAD = 4 * BLOCK
WIDE = RPL * BLOCK

HIGH = lax.Precision.HIGHEST
AXES = ("mesh", "grp")


def split(x):
    high = x.astype(jnp.bfloat16)
    low = (x - high.astype(jnp.float32)).astype(jnp.bfloat16)
    return high, low


def dot(a, b, dims=((1,), (0,))):
    return lax.dot_general(a, b, (dims, ((), ())), preferred_element_type=jnp.float32)


def dot3(a, b_high, b_low, dims=((1,), (0,))):
    a_high, a_low = split(a)
    return dot(a_high, b_high, dims) + (dot(a_low, b_high, dims) + dot(a_high, b_low, dims))


def first_half():
    return lax.broadcasted_iota(jnp.int32, (S, PAIR), 1) < BLOCK


def turned(tile):
    return pltpu.roll(tile, BLOCK, 1)


def doubled(tile):
    first = first_half()
    other = turned(tile)
    return jnp.where(first, tile, other), jnp.where(first, other, tile)


def parity_of(index):
    return jnp.bitwise_and(index, 1)


def pair_tile(ref, block):
    start = pl.multiple_of(lax.shift_right_logical(block, 1) * PAIR, PAIR)
    return pl.ds(start, PAIR)


def in_half(tile, block, half):
    return jnp.where(parity_of(block) == half, tile, turned(tile))


def listed(halo, level, ref):
    tiles = []
    first = first_half()
    for pair in range(HB // 2):
        h = [halo[2 * pair + half, level] for half in range(2)]
        moved = [in_half(ref[:, pair_tile(ref, h[half])], h[half], half) for half in range(2)]
        tiles.append(jnp.where(first, moved[0], moved[1]))
    return jnp.concatenate(tiles, axis=1)


def own_blocks(out):
    first = first_half()
    rows = [out[j * S : (j + 1) * S] for j in range(4)]
    return jnp.concatenate(
        [
            jnp.where(first, rows[0][:, :PAIR], rows[1][:, :PAIR]),
            jnp.where(first, rows[2][:, PAIR:], rows[3][:, PAIR:]),
        ],
        axis=1,
    )


def spread(quad):
    lane = lax.shift_right_logical(lax.broadcasted_iota(jnp.int32, (S, QUAD), 1), 6)
    return jnp.concatenate([jnp.where(lane == j, quad, 0.0) for j in range(4)], axis=0)


def stacked(quad):
    parts = []
    for pair in range(2):
        tile = quad[:, pair * PAIR : (pair + 1) * PAIR]
        parts += [tile[:, :BLOCK], turned(tile)[:, :BLOCK]]
    return jnp.concatenate(parts, axis=0)


def parity():
    return parity_of(lax.axis_index("grp"))


def prepare_kernel(level, plan, halo, forcing, inverse, out, *send):
    for quad in range(2):
        lanes = slice(quad * QUAD, (quad + 1) * QUAD)
        rows = []
        for j in range(4):
            block = plan[0, level * RPL + 4 * quad + j]
            tile = forcing[:, pair_tile(forcing, block)]
            rows.append(in_half(tile, block, 0)[:, :BLOCK])
        out[:, lanes] = own_blocks(dot3(jnp.concatenate(rows, axis=0), *split(inverse[:, lanes])))
    if send:
        send[0][...] = listed(halo, level, out)


def compose_kernel(blocks, inverse, high, low):
    lane = lax.shift_right_logical(lax.broadcasted_iota(jnp.int32, (BLOCK, QUAD), 1), 6)
    for quad in range(2):
        lanes = slice(quad * QUAD, (quad + 1) * QUAD)
        inv = inverse[:, lanes]
        diagonal = jnp.concatenate([jnp.where(lane == j, inv, 0.0) for j in range(4)], axis=0)
        d_high, d_low = split(diagonal)
        product = dot3(blocks[:, lanes], d_high, d_low)
        p_high, p_low = split(product)
        high[:, lanes] = p_high
        low[:, lanes] = p_low


def combine_kernel(level, halo, x, y, w, diag, inverse, out, *send):
    for quad in range(2):
        lanes = slice(quad * QUAD, (quad + 1) * QUAD)
        value = x[:, lanes]
        image = own_blocks(dot3(stacked(value), *split(diag[:, lanes])))
        image = own_blocks(dot3(stacked(image), *split(inverse[:, lanes])))
        out[:, lanes] = 2.0 * value + y[:, lanes] - w[:, lanes] - image
    if send:
        send[0][...] = listed(halo, level, out)


def fill_slots(slots, prev, swap0, swap1):
    for pair in range(RPL // 2):
        a, b = doubled(prev[:, pair * PAIR : (pair + 1) * PAIR])
        slots[2 * pair] = a
        slots[2 * pair + 1] = b
    odd = parity()
    for ref, base in ((swap1, RPL + HB * odd), (swap0, RPL + HB - HB * odd)):
        for pair in range(HB // 2):
            a, b = doubled(ref[:, pair * PAIR : (pair + 1) * PAIR])
            slots[base + 2 * pair] = a
            slots[base + 2 * pair + 1] = b


def gather_kernel(row, level, columns, halo, base, high, low, prev, swap0, swap1, out, *rest):
    slots = rest[-1]
    fill_slots(slots, prev, swap0, swap1)
    first = first_half()
    for quad in range(2):
        rows = []
        for j in range(4):
            c = [columns[k, row * RPL + quad * 4 + j] for k in range(KL)]
            rows.append(
                jnp.concatenate(
                    [
                        jnp.where(first, slots[c[0]], slots[c[1]]),
                        jnp.where(first, slots[c[2]], slots[c[3]]),
                    ],
                    axis=1,
                )
            )
        lanes = slice(quad * QUAD, (quad + 1) * QUAD)
        product = dot3(jnp.concatenate(rows, axis=0), high[:, lanes], low[:, lanes])
        out[:, lanes] = base[:, lanes] - own_blocks(product)
    if len(rest) > 1:
        rest[0][...] = listed(halo, level, out)


def add_listed(halo, level, out, arriving):
    first = first_half()
    for i in range(HB):
        h = halo[i, level]
        tile = arriving[:, (i // 2) * PAIR : (i // 2 + 1) * PAIR]
        tile = jnp.where(parity_of(h) == i % 2, tile, turned(tile))
        keep = first == (parity_of(h) == 0)
        lanes = pair_tile(out, h)
        out[:, lanes] = out[:, lanes] - jnp.where(keep, tile, 0.0)


def push_kernel(row, level, parts, columns, halo, *refs):
    refs = list(refs)
    source = refs.pop(0)
    if halo is not None:
        own_in, swap0, swap1 = [refs.pop(0) for _ in range(3)]
    if columns is not None:
        high, low = refs.pop(0), refs.pop(0)
    if parts:
        total = refs.pop(0)[...]
        for _ in range(parts - 1):
            total = total + refs.pop(0)[...]
    if halo is not None:
        out = refs.pop(0)
        out[...] = source[...] - own_in[...]
        add_listed(halo, level, out, swap0[...] + swap1[...])
    else:
        out = source
    if columns is None:
        return
    own, send0, send1 = refs[:3]
    slots = refs[-1]
    if parts:
        refs[3][...] = total
    slots[...] = jnp.zeros_like(slots)
    first = first_half()
    for quad in range(2):
        lanes = slice(quad * QUAD, (quad + 1) * QUAD)
        terms = dot3(spread(out[:, lanes]), high[:, lanes], low[:, lanes], ((1,), (1,)))
        for j in range(4):
            for k in range(KL):
                c = columns[k, row * RPL + quad * 4 + j]
                tile = terms[j * S : (j + 1) * S, (k // 2) * PAIR : (k // 2 + 1) * PAIR]
                keep = first if k % 2 == 0 else jnp.logical_not(first)
                slots[c] += jnp.where(keep, tile, 0.0)

    def both_halves(c):
        value = slots[c]
        return value + turned(value)

    for pair in range(RPL // 2):
        own[:, pair * PAIR : (pair + 1) * PAIR] = jnp.where(
            first, both_halves(2 * pair), both_halves(2 * pair + 1)
        )
    odd = parity()
    for ref, base in ((send1, RPL + HB * odd), (send0, RPL + HB - HB * odd)):
        for pair in range(HB // 2):
            ref[:, pair * PAIR : (pair + 1) * PAIR] = jnp.where(
                first, both_halves(base + 2 * pair), both_halves(base + 2 * pair + 1)
            )


def place(natural, block, piece, first):
    keep = first == (parity_of(block) == 0)
    lanes = pair_tile(natural, block)
    natural[:, lanes] = jnp.where(keep, piece, natural[:, lanes])


def full_dot(a, b, dims=((1,), (0,))):
    return lax.dot_general(a, b, (dims, ((), ())), precision=HIGH, preferred_element_type=jnp.float32)


def finish_kernel(plan, turn, inverse, *refs):
    fields, out, natural = refs[:LEV], refs[LEV], refs[LEV + 1]
    first = first_half()
    for level in range(LEV):
        for quad in range(2):
            i_high, i_low = split(inverse[:, level * WIDE + quad * QUAD : level * WIDE + (quad + 1) * QUAD])
            value = fields[level][:, quad * QUAD : (quad + 1) * QUAD]
            product = dot3(spread(value), i_high, i_low, ((1,), (1,)))
            for j in range(4):
                block = plan[0, level * RPL + 4 * quad + j]
                piece = product[j * S : (j + 1) * S]
                place(natural, block, jnp.concatenate([piece, piece], axis=1), first)
    out[...] = full_dot(turn[...], natural[...])


def basis_kernel(plan, turn, *refs):
    fields, out, natural = refs[:LEV], refs[LEV], refs[LEV + 1]
    first = first_half()
    for level in range(LEV):
        for pair in range(RPL // 2):
            a, b = doubled(fields[level][:, pair * PAIR : (pair + 1) * PAIR])
            at = level * RPL + 2 * pair
            place(natural, plan[0, at], a, first)
            place(natural, plan[0, at + 1], b, first)
    out[...] = full_dot(turn[...], natural[...])


def gram_kernel(*refs):
    fields, out = refs[:LEV], refs[-1]
    total = full_dot(fields[0][...], fields[0][...], ((1,), (1,)))
    for field in fields[1:]:
        total = total + full_dot(field[...], field[...], ((1,), (1,)))
    out[...] = total


def factor_kernel(scale, gram, out):
    row = lax.broadcasted_iota(jnp.int32, (S, S), 0)
    unit = jnp.where(row == lax.broadcasted_iota(jnp.int32, (S, S), 1), 1.0, 0.0)
    table = jnp.concatenate([gram[...], unit], axis=1)
    below = lax.broadcasted_iota(jnp.int32, (S, 1), 0)
    pivots = jnp.ones((S, 1), jnp.float32)
    for k in range(S):
        pivot = table[k : k + 1, k : k + 1]
        pivots = jnp.where(below == k, pivot, pivots)
        factor = jnp.where(below > k, table[:, k : k + 1] / pivot, 0.0)
        table = table - factor * table[k : k + 1, :]
    out[...] = table[:, S:] * (scale / jnp.sqrt(pivots))


def ortho_kernel(turn, *refs):
    fields, outs, gram = refs[:LEV], refs[-LEV - 1 : -1], refs[-1]
    total = None
    for field, out in zip(fields, outs):
        value = full_dot(turn[...], field[...])
        out[...] = value
        part = full_dot(value, value, ((1,), (1,)))
        total = part if total is None else total + part
    gram[...] = total


SMEM_SPEC = pl.BlockSpec(memory_space=pltpu.SMEM)
VMEM_SPEC = pl.BlockSpec(memory_space=pltpu.VMEM)
ANY_SPEC = pl.BlockSpec(memory_space=pl.ANY)


def part(shape, place):
    return pl.BlockSpec(shape, lambda _: place)


def call(kernel, operands, outs, scratch=(), flops=0, after=None, vmem=6):
    name = getattr(kernel, "func", kernel).__name__
    pairs = [o if isinstance(o, tuple) else (o, VMEM_SPEC) for o in operands]
    if after is not None:
        inner, at = kernel, len(pairs)
        kernel = lambda *refs: inner(*refs[:at], *refs[at + 1 :])
        pairs.append((after, ANY_SPEC))
    moved = 4 * sum(math.prod(shape) for shape, _ in outs) * 2
    return pl.pallas_call(
        kernel,
        out_shape=[jax.ShapeDtypeStruct(shape, dtype) for shape, dtype in outs],
        grid=(1,) if any(spec.block_shape is not None for _, spec in pairs) else (),
        in_specs=[spec for _, spec in pairs],
        out_specs=[VMEM_SPEC] * len(outs),
        scratch_shapes=list(scratch),
        name=name,
        compiler_params=pltpu.CompilerParams(vmem_limit_bytes=vmem * 1024 * 1024),
        cost_estimate=pl.CostEstimate(flops=flops, bytes_accessed=moved, transcendentals=0),
    )(*[array for array, _ in pairs])


F32 = jnp.float32
BF16 = jnp.bfloat16
LEVEL_FIELD = ((S, WIDE), F32)
SENT = ((S, HB * BLOCK), F32)
SLOTS = pltpu.VMEM((RPL + 2 * HB, S, PAIR), F32)


def swap(sent0, sent1):
    count = lax.axis_size(AXES)
    even = [(i, i ^ 1) for i in range(count)]
    other = [((i + 1) ^ 1) - 1 for i in range(count)]
    odd = [(i, j) for i, j in enumerate(other) if 0 <= j < count]
    swap1 = lax.ppermute(sent1, AXES, odd)
    swap0 = lax.ppermute(sent0, AXES, even)
    return swap0, swap1


def shards(forcing, plan, lower_blocks, lower_columns, upper_blocks, upper_columns, diag_blocks, inverse_blocks, halo_list):
    smem = lambda array: (array, SMEM_SPEC)
    plan = smem(plan)
    halo = smem(halo_list.T)
    lower_columns = smem(lower_columns.T)
    upper_columns = smem(upper_columns.T)
    square_at = lambda array, level: (array, part((BLOCK, WIDE), (0, level)))
    inverse = [square_at(inverse_blocks, level) for level in range(LEV)]
    diagonal = [square_at(diag_blocks, level) for level in range(LEV)]

    def prepare(level, after=None):
        return call(
            functools.partial(prepare_kernel, level),
            [plan, halo, forcing, inverse[level]],
            [LEVEL_FIELD, SENT] if level == 0 else [LEVEL_FIELD],
            after=after,
        )

    def compose(blocks, level, row):
        wide = ((KL * BLOCK, WIDE), BF16)
        tall = (blocks, part((KL * BLOCK, WIDE), (0, level)))
        return call(compose_kernel, [tall, inverse[row]], [wide, wide], flops=2 * 6 * 256**3)

    y0, sent = prepare(0)
    y = [y0] + [prepare(level, sent)[0] for level in range(1, LEV)]
    lower = [compose(lower_blocks, level, level + 1) for level in range(LEV - 1)]
    upper = [compose(upper_blocks, level, level) for level in range(LEV - 1)]

    def gather(base, blocks, columns, row, level, prev, sent, send_on):
        swap0, swap1 = swap(sent, sent)
        outs = call(
            functools.partial(gather_kernel, row, level),
            [columns, halo, base, *blocks, prev, swap0, swap1],
            [LEVEL_FIELD, SENT] if send_on else [LEVEL_FIELD],
            [SLOTS],
        )
        return (outs[0], outs[1]) if send_on else (outs[0], None)

    def ascend(base, sent):
        field = [base[0]]
        for level in range(1, LEV):
            value, sent = gather(
                base[level], lower[level - 1], lower_columns, level - 1, level, field[-1], sent, True
            )
            field.append(value)
        return field, sent

    def descend(base, sent):
        field = [None] * LEV
        field[LEV - 1] = base[LEV - 1]
        for level in range(LEV - 2, -1, -1):
            field[level], sent = gather(
                base[level], upper[level], upper_columns, level, level, field[level + 1], sent, level > 0
            )
        return field

    w, sent = ascend(y, sent)
    x = descend(w, sent)

    def combine(level):
        return call(
            functools.partial(combine_kernel, level),
            [halo, x[level], y[level], w[level], diagonal[level], inverse[level]],
            [LEVEL_FIELD, SENT] if level == 0 else [LEVEL_FIELD],
        )

    c0, sent = combine(0)
    c = [c0] + [combine(level)[0] for level in range(1, LEV)]
    v, sent = ascend(c, sent)
    sketch = descend([v[level] + w[level] - x[level] for level in range(LEV)], sent)

    count = lax.axis_size(AXES)
    square = ((S, S), F32)

    def push(source, row, level, columns, blocks, arrived, parts=(), after=None):
        kernel = functools.partial(push_kernel, row, level, len(parts))
        operands = [source]
        if arrived is None:
            kernel = functools.partial(push_kernel, row, level, len(parts))
            bound = lambda columns, *refs: kernel(columns, None, *refs)
            operands = [columns, *operands, *blocks, *parts]
            outs = []
        elif columns is None:
            bound = lambda halo, *refs: kernel(None, halo, *refs)
            operands = [halo, *operands, *arrived, *parts]
            outs = [LEVEL_FIELD]
        else:
            bound = lambda columns, halo, *refs: kernel(columns, halo, *refs)
            operands = [columns, halo, *operands, *arrived, *blocks, *parts]
            outs = [LEVEL_FIELD]
        bound.__name__ = "push_kernel"
        if columns is not None:
            outs = outs + [LEVEL_FIELD, SENT, SENT] + ([square] if parts else [])
        results = list(call(bound, operands, outs, [SLOTS] if columns is not None else [], after=after))
        value = source if arrived is None else results.pop(0)
        if columns is None:
            return value, None, None
        total = results.pop(3) if parts else None
        return value, (results[0], *swap(results[1], results[2])), total

    def from_partners(part, distances):
        return [part] + [lax.ppermute(part, AXES, [(i, i ^ far) for i in range(count)]) for far in distances]

    steps = [(1, 2, 3), (4,), (8,), (16,), (32,), (64,)]
    levels = [(level, level, upper_columns, upper) for level in range(LEV - 1)]
    levels += [(level, level - 1, lower_columns, lower) for level in range(LEV - 1, 0, -1)]
    before = [None] * LEV
    turned_back = [None] * LEV
    arrived = None
    parts, after = (), None
    for turn, (level, row, columns, blocks) in enumerate(levels):
        rising = turn < LEV - 1
        source = sketch[level] if turn < LEV else before[level]
        value, arrived, total = push(source, row, level, columns, blocks[row], arrived, parts, after)
        (before if rising else turned_back)[level] = value
        if turn == LEV - 1:
            before[level] = value
        step = turn % (LEV - 1)
        parts, after = (), None
        if turn == 0:
            total = call(gram_kernel, sketch, [square], after=arrived[0])[0]
        if turn == LEV - 1:
            *ortho, total = call(ortho_kernel, [first, *sketch], [LEVEL_FIELD] * LEV + [square], after=arrived[0])
        if step < LEV - 2:
            parts = from_partners(total, steps[step])
        elif rising:
            first = after = call(functools.partial(factor_kernel, 1.0), [total], [square])[0]
        else:
            scale = math.sqrt(NB * BLOCK * count)
            second = call(functools.partial(factor_kernel, scale), [total], [square])[0]
    natural = [((S, NB * BLOCK), F32)]
    room = [pltpu.VMEM((S, NB * BLOCK), F32)]
    basis = call(basis_kernel, [plan, second, *ortho], natural, room)[0]
    both = jnp.dot(second, first, precision=HIGH)
    turned_back[0], _, _ = push(before[0], 0, 0, None, None, arrived, (), basis)
    adjoint_field = call(
        finish_kernel, [plan, both, inverse_blocks, *turned_back], natural, room
    )[0]
    return (basis, adjoint_field)


def solution(mesh):
    in_specs = (
        P(None, AXES),
        P(AXES, None),
        P(None, AXES),
        P(AXES, None),
        P(None, AXES),
        P(AXES, None),
        P(None, AXES),
        P(None, AXES),
        P(AXES, None),
    )
    out_specs = (P(None, AXES), P(None, AXES))
    return jax.shard_map(shards, mesh=mesh, in_specs=in_specs, out_specs=out_specs, check_vma=False)
```

```python
import functools
import math

import jax
import jax.numpy as jnp
from jax import lax
from jax.experimental import pallas as pl
from jax.experimental.pallas import tpu as pltpu
from jax.sharding import PartitionSpec as P

S = 32
BLOCK = 64
KL = 4
LEV = 8
RPL = 8
HB = 4
NB = 64
PAIR = 2 * BLOCK
QUAD = 4 * BLOCK
WIDE = RPL * BLOCK

HIGH = lax.Precision.HIGHEST
AXES = ("mesh", "grp")


def split(x):
    high = x.astype(jnp.bfloat16)
    low = (x - high.astype(jnp.float32)).astype(jnp.bfloat16)
    return high, low


def dot(a, b, dims=((1,), (0,))):
    return lax.dot_general(a, b, (dims, ((), ())), preferred_element_type=jnp.float32)


def dot3(a, b_high, b_low, dims=((1,), (0,))):
    a_high, a_low = split(a)
    return dot(a_high, b_high, dims) + (dot(a_low, b_high, dims) + dot(a_high, b_low, dims))


def first_half():
    return lax.broadcasted_iota(jnp.int32, (S, PAIR), 1) < BLOCK


def turned(tile):
    return pltpu.roll(tile, BLOCK, 1)


def doubled(tile):
    first = first_half()
    other = turned(tile)
    return jnp.where(first, tile, other), jnp.where(first, other, tile)


def parity_of(index):
    return jnp.bitwise_and(index, 1)


def pair_tile(ref, block):
    start = pl.multiple_of(lax.shift_right_logical(block, 1) * PAIR, PAIR)
    return pl.ds(start, PAIR)


def in_half(tile, block, half):
    return jnp.where(parity_of(block) == half, tile, turned(tile))


def listed(halo, level, ref):
    tiles = []
    first = first_half()
    for pair in range(HB // 2):
        h = [halo[2 * pair + half, level] for half in range(2)]
        moved = [in_half(ref[:, pair_tile(ref, h[half])], h[half], half) for half in range(2)]
        tiles.append(jnp.where(first, moved[0], moved[1]))
    return jnp.concatenate(tiles, axis=1)


def own_blocks(out):
    first = first_half()
    rows = [out[j * S : (j + 1) * S] for j in range(4)]
    return jnp.concatenate(
        [
            jnp.where(first, rows[0][:, :PAIR], rows[1][:, :PAIR]),
            jnp.where(first, rows[2][:, PAIR:], rows[3][:, PAIR:]),
        ],
        axis=1,
    )


def spread(quad):
    lane = lax.shift_right_logical(lax.broadcasted_iota(jnp.int32, (S, QUAD), 1), 6)
    return jnp.concatenate([jnp.where(lane == j, quad, 0.0) for j in range(4)], axis=0)


def stacked(quad):
    parts = []
    for pair in range(2):
        tile = quad[:, pair * PAIR : (pair + 1) * PAIR]
        parts += [tile[:, :BLOCK], turned(tile)[:, :BLOCK]]
    return jnp.concatenate(parts, axis=0)


def from_neighbour(swap1, spare):
    last = lax.axis_size("mesh") * lax.axis_size("grp") - 1
    place = lax.axis_index("mesh") * lax.axis_size("grp") + lax.axis_index("grp")
    end = jnp.logical_or(place == 0, place == last)
    beside = jnp.logical_or(place == 1, place == last - 1)
    return jnp.where(end, 0.0, jnp.where(beside, spare[...], swap1[...]))


def parity():
    return parity_of(lax.axis_index("grp"))


def prepare_kernel(level, plan, halo, forcing, inverse, out, *send):
    plan, halo = plan[...], halo[...]
    for quad in range(2):
        lanes = slice(quad * QUAD, (quad + 1) * QUAD)
        rows = []
        for j in range(4):
            block = plan[0, level * RPL + 4 * quad + j]
            tile = forcing[:, pair_tile(forcing, block)]
            rows.append(in_half(tile, block, 0)[:, :BLOCK])
        out[:, lanes] = own_blocks(dot3(jnp.concatenate(rows, axis=0), *split(inverse[:, lanes])))
    if send:
        send[0][...] = listed(halo, level, out)


def compose_kernel(blocks, inverse, high, low):
    lane = lax.shift_right_logical(lax.broadcasted_iota(jnp.int32, (BLOCK, QUAD), 1), 6)
    for quad in range(2):
        lanes = slice(quad * QUAD, (quad + 1) * QUAD)
        inv = inverse[:, lanes]
        diagonal = jnp.concatenate([jnp.where(lane == j, inv, 0.0) for j in range(4)], axis=0)
        d_high, d_low = split(diagonal)
        product = dot3(blocks[:, lanes], d_high, d_low)
        p_high, p_low = split(product)
        high[:, lanes] = p_high
        low[:, lanes] = p_low


def combine_kernel(level, halo, x, y, w, diag, inverse, out, *send):
    halo = halo[...]
    for quad in range(2):
        lanes = slice(quad * QUAD, (quad + 1) * QUAD)
        value = x[:, lanes]
        image = own_blocks(dot3(stacked(value), *split(diag[:, lanes])))
        image = own_blocks(dot3(stacked(image), *split(inverse[:, lanes])))
        out[:, lanes] = 2.0 * value + y[:, lanes] - w[:, lanes] - image
    if send:
        send[0][...] = listed(halo, level, out)


def fill_slots(slots, prev, swap0, swap1, spare):
    for pair in range(RPL // 2):
        a, b = doubled(prev[:, pair * PAIR : (pair + 1) * PAIR])
        slots[2 * pair] = a
        slots[2 * pair + 1] = b
    odd = parity()
    for ref, base in ((from_neighbour(swap1, spare), RPL + HB * odd), (swap0, RPL + HB - HB * odd)):
        for pair in range(HB // 2):
            a, b = doubled(ref[:, pair * PAIR : (pair + 1) * PAIR])
            slots[base + 2 * pair] = a
            slots[base + 2 * pair + 1] = b


def gather_kernel(row, level, columns, halo, base, high, low, prev, swap0, swap1, spare, out, *rest):
    columns, halo = columns[...], halo[...]
    slots = rest[-1]
    fill_slots(slots, prev, swap0, swap1, spare)
    first = first_half()
    for quad in range(2):
        rows = []
        for j in range(4):
            c = [columns[k, row * RPL + quad * 4 + j] for k in range(KL)]
            rows.append(
                jnp.concatenate(
                    [
                        jnp.where(first, slots[c[0]], slots[c[1]]),
                        jnp.where(first, slots[c[2]], slots[c[3]]),
                    ],
                    axis=1,
                )
            )
        lanes = slice(quad * QUAD, (quad + 1) * QUAD)
        product = dot3(jnp.concatenate(rows, axis=0), high[:, lanes], low[:, lanes])
        out[:, lanes] = base[:, lanes] - own_blocks(product)
    if len(rest) > 1:
        rest[0][...] = listed(halo, level, out)


def add_listed(halo, level, out, arriving):
    first = first_half()
    for i in range(HB):
        h = halo[i, level]
        tile = arriving[:, (i // 2) * PAIR : (i // 2 + 1) * PAIR]
        tile = jnp.where(parity_of(h) == i % 2, tile, turned(tile))
        keep = first == (parity_of(h) == 0)
        lanes = pair_tile(out, h)
        out[:, lanes] = out[:, lanes] - jnp.where(keep, tile, 0.0)


def push_kernel(row, level, parts, columns, halo, *refs):
    refs = list(refs)
    source = refs.pop(0)
    if halo is not None:
        halo = halo[...]
        own_in, swap0, swap1, spare = [refs.pop(0) for _ in range(4)]
    if columns is not None:
        columns = columns[...]
        high, low = refs.pop(0), refs.pop(0)
    if parts:
        total = refs.pop(0)[...]
        for _ in range(parts - 1):
            total = total + refs.pop(0)[...]
    if halo is not None:
        out = refs.pop(0)
        out[...] = source[...] - own_in[...]
        add_listed(halo, level, out, swap0[...] + from_neighbour(swap1, spare))
    else:
        out = source
    if columns is None:
        return
    own, send0, send1 = refs[:3]
    halves = refs[-1]
    if parts:
        refs[3][...] = total
    halves[...] = jnp.zeros_like(halves)
    first = first_half()
    for quad in range(2):
        lanes = slice(quad * QUAD, (quad + 1) * QUAD)
        terms = dot3(spread(out[:, lanes]), high[:, lanes], low[:, lanes], ((1,), (1,)))
        for j in range(4):
            for k in range(KL):
                c = columns[k, row * RPL + quad * 4 + j]
                tile = terms[j * S : (j + 1) * S, (k // 2) * PAIR : (k // 2 + 1) * PAIR]
                halves[k % 2, c] += tile

    def both_halves(c):
        value = jnp.where(first, halves[0, c], halves[1, c])
        return value + turned(value)

    for pair in range(RPL // 2):
        own[:, pair * PAIR : (pair + 1) * PAIR] = jnp.where(
            first, both_halves(2 * pair), both_halves(2 * pair + 1)
        )
    odd = parity()
    for ref, base in ((send1, RPL + HB * odd), (send0, RPL + HB - HB * odd)):
        for pair in range(HB // 2):
            ref[:, pair * PAIR : (pair + 1) * PAIR] = jnp.where(
                first, both_halves(base + 2 * pair), both_halves(base + 2 * pair + 1)
            )


def place(natural, block, piece, first):
    keep = first == (parity_of(block) == 0)
    lanes = pair_tile(natural, block)
    natural[:, lanes] = jnp.where(keep, piece, natural[:, lanes])


def full_dot(a, b, dims=((1,), (0,))):
    return lax.dot_general(a, b, (dims, ((), ())), precision=HIGH, preferred_element_type=jnp.float32)


def finish_kernel(plan, turn, inverse, *refs):
    plan = plan[...]
    fields, out, natural = refs[:LEV], refs[LEV], refs[LEV + 1]
    first = first_half()
    for level in range(LEV):
        for quad in range(2):
            i_high, i_low = split(inverse[:, level * WIDE + quad * QUAD : level * WIDE + (quad + 1) * QUAD])
            value = fields[level][:, quad * QUAD : (quad + 1) * QUAD]
            product = dot3(spread(value), i_high, i_low, ((1,), (1,)))
            for j in range(4):
                block = plan[0, level * RPL + 4 * quad + j]
                piece = product[j * S : (j + 1) * S]
                place(natural, block, jnp.concatenate([piece, piece], axis=1), first)
    out[...] = full_dot(turn[...], natural[...])


def basis_kernel(plan, turn, *refs):
    plan = plan[...]
    fields, out, natural = refs[:LEV], refs[LEV], refs[LEV + 1]
    first = first_half()
    for level in range(LEV):
        for pair in range(RPL // 2):
            a, b = doubled(fields[level][:, pair * PAIR : (pair + 1) * PAIR])
            at = level * RPL + 2 * pair
            place(natural, plan[0, at], a, first)
            place(natural, plan[0, at + 1], b, first)
    out[...] = full_dot(turn[...], natural[...])


def gram_kernel(*refs):
    fields, out = refs[:LEV], refs[-1]
    total = full_dot(fields[0][...], fields[0][...], ((1,), (1,)))
    for field in fields[1:]:
        total = total + full_dot(field[...], field[...], ((1,), (1,)))
    out[...] = total


def factor_kernel(scale, gram, out):
    row = lax.broadcasted_iota(jnp.int32, (S, S), 0)
    unit = jnp.where(row == lax.broadcasted_iota(jnp.int32, (S, S), 1), 1.0, 0.0)
    table = jnp.concatenate([gram[...], unit], axis=1)
    below = lax.broadcasted_iota(jnp.int32, (S, 1), 0)
    pivots = jnp.ones((S, 1), jnp.float32)
    for k in range(S):
        pivot = table[k : k + 1, k : k + 1]
        pivots = jnp.where(below == k, pivot, pivots)
        factor = jnp.where(below > k, table[:, k : k + 1] / pivot, 0.0)
        table = table - factor * table[k : k + 1, :]
    out[...] = table[:, S:] * (scale / jnp.sqrt(pivots))


def ortho_kernel(turn, *refs):
    fields, outs, gram = refs[:LEV], refs[-LEV - 1 : -1], refs[-1]
    total = None
    for field, out in zip(fields, outs):
        value = full_dot(turn[...], field[...])
        out[...] = value
        part = full_dot(value, value, ((1,), (1,)))
        total = part if total is None else total + part
    gram[...] = total


VMEM_SPEC = pl.BlockSpec(memory_space=pltpu.VMEM)
ANY_SPEC = pl.BlockSpec(memory_space=pl.ANY)


def part(shape, place):
    return pl.BlockSpec(shape, lambda _: place)


def call(kernel, operands, outs, scratch=(), flops=0, after=None, vmem=6):
    name = getattr(kernel, "func", kernel).__name__
    pairs = [o if isinstance(o, tuple) else (o, VMEM_SPEC) for o in operands]
    if after is not None:
        inner, at = kernel, len(pairs)
        kernel = lambda *refs: inner(*refs[:at], *refs[at + 1 :])
        pairs.append((after, ANY_SPEC))
    moved = 4 * sum(math.prod(shape) for shape, _ in outs) * 2
    return pl.pallas_call(
        kernel,
        out_shape=[jax.ShapeDtypeStruct(shape, dtype) for shape, dtype in outs],
        grid=(1,) if any(spec.block_shape is not None for _, spec in pairs) else (),
        in_specs=[spec for _, spec in pairs],
        out_specs=[VMEM_SPEC] * len(outs),
        scratch_shapes=list(scratch),
        name=name,
        compiler_params=pltpu.CompilerParams(vmem_limit_bytes=vmem * 1024 * 1024),
        cost_estimate=pl.CostEstimate(flops=flops, bytes_accessed=moved, transcendentals=0),
    )(*[array for array, _ in pairs])


F32 = jnp.float32
BF16 = jnp.bfloat16
LEVEL_FIELD = ((S, WIDE), F32)
SENT = ((S, HB * BLOCK), F32)
SLOTS = pltpu.VMEM((RPL + 2 * HB, S, PAIR), F32)
HALVES = pltpu.VMEM((2, RPL + 2 * HB, S, PAIR), F32)


def swap(sent0, sent1):
    count = lax.axis_size(AXES)
    last = count - 1
    even = {i: i ^ 1 for i in range(count)}
    odd = {i: ((i + 1) ^ 1) - 1 for i in range(count)}
    odd.update({1: 2, 2: 0, 0: 1})
    odd.update({last - 1: last - 2, last - 2: last, last: last - 1})
    core = {i: i ^ 4 for i in range(count)}
    for start, end in ((2, 1), (last - 2, last - 1)):
        core.update({start: end, end: end ^ 4, end ^ 4: start ^ 4, start ^ 4: start})
    swap0 = lax.ppermute(sent0, AXES, sorted(even.items()))
    spare = lax.ppermute(sent1, AXES, sorted(core.items()))
    swap1 = lax.ppermute(sent1, AXES, sorted(odd.items()))
    return swap0, swap1, spare


def shards(forcing, plan, lower_blocks, lower_columns, upper_blocks, upper_columns, diag_blocks, inverse_blocks, halo_list):
    halo = halo_list.T
    lower_columns = lower_columns.T
    upper_columns = upper_columns.T
    square_at = lambda array, level: (array, part((BLOCK, WIDE), (0, level)))
    inverse = [square_at(inverse_blocks, level) for level in range(LEV)]
    diagonal = [square_at(diag_blocks, level) for level in range(LEV)]

    def prepare(level, after=None):
        return call(
            functools.partial(prepare_kernel, level),
            [plan, halo, forcing, inverse[level]],
            [LEVEL_FIELD, SENT] if level == 0 else [LEVEL_FIELD],
            after=after,
        )

    def compose(blocks, level, row):
        wide = ((KL * BLOCK, WIDE), BF16)
        tall = (blocks, part((KL * BLOCK, WIDE), (0, level)))
        return call(compose_kernel, [tall, inverse[row]], [wide, wide], flops=2 * 6 * 256**3)

    y0, sent = prepare(0)
    y = [y0] + [prepare(level, sent)[0] for level in range(1, LEV)]
    lower = [compose(lower_blocks, level, level + 1) for level in range(LEV - 1)]
    upper = [compose(upper_blocks, level, level) for level in range(LEV - 1)]

    def gather(base, blocks, columns, row, level, prev, sent, send_on):
        swaps = swap(sent, sent)
        outs = call(
            functools.partial(gather_kernel, row, level),
            [columns, halo, base, *blocks, prev, *swaps],
            [LEVEL_FIELD, SENT] if send_on else [LEVEL_FIELD],
            [SLOTS],
        )
        return (outs[0], outs[1]) if send_on else (outs[0], None)

    def ascend(base, sent):
        field = [base[0]]
        for level in range(1, LEV):
            value, sent = gather(
                base[level], lower[level - 1], lower_columns, level - 1, level, field[-1], sent, True
            )
            field.append(value)
        return field, sent

    def descend(base, sent):
        field = [None] * LEV
        field[LEV - 1] = base[LEV - 1]
        for level in range(LEV - 2, -1, -1):
            field[level], sent = gather(
                base[level], upper[level], upper_columns, level, level, field[level + 1], sent, level > 0
            )
        return field

    w, sent = ascend(y, sent)
    x = descend(w, sent)

    def combine(level):
        return call(
            functools.partial(combine_kernel, level),
            [halo, x[level], y[level], w[level], diagonal[level], inverse[level]],
            [LEVEL_FIELD, SENT] if level == 0 else [LEVEL_FIELD],
        )

    c0, sent = combine(0)
    c = [c0] + [combine(level)[0] for level in range(1, LEV)]
    v, sent = ascend(c, sent)
    sketch = descend([v[level] + w[level] - x[level] for level in range(LEV)], sent)

    count = lax.axis_size(AXES)
    square = ((S, S), F32)

    def push(source, row, level, columns, blocks, arrived, parts=(), after=None):
        kernel = functools.partial(push_kernel, row, level, len(parts))
        operands = [source]
        if arrived is None:
            kernel = functools.partial(push_kernel, row, level, len(parts))
            bound = lambda columns, *refs: kernel(columns, None, *refs)
            operands = [columns, *operands, *blocks, *parts]
            outs = []
        elif columns is None:
            bound = lambda halo, *refs: kernel(None, halo, *refs)
            operands = [halo, *operands, *arrived, *parts]
            outs = [LEVEL_FIELD]
        else:
            bound = lambda columns, halo, *refs: kernel(columns, halo, *refs)
            operands = [columns, halo, *operands, *arrived, *blocks, *parts]
            outs = [LEVEL_FIELD]
        bound.__name__ = "push_kernel"
        if columns is not None:
            outs = outs + [LEVEL_FIELD, SENT, SENT] + ([square] if parts else [])
        results = list(call(bound, operands, outs, [HALVES] if columns is not None else [], after=after))
        value = source if arrived is None else results.pop(0)
        if columns is None:
            return value, None, None
        total = results.pop(3) if parts else None
        return value, (results[0], *swap(results[1], results[2])), total

    def from_partners(part, distances):
        return [part] + [lax.ppermute(part, AXES, [(i, i ^ far) for i in range(count)]) for far in distances]

    steps = [(1, 2, 3), (4,), (8,), (16,), (32,), (64,)]
    levels = [(level, level, upper_columns, upper) for level in range(LEV - 1)]
    levels += [(level, level - 1, lower_columns, lower) for level in range(LEV - 1, 0, -1)]
    before = [None] * LEV
    turned_back = [None] * LEV
    arrived = None
    parts, after = (), None
    for turn, (level, row, columns, blocks) in enumerate(levels):
        rising = turn < LEV - 1
        source = sketch[level] if turn < LEV else before[level]
        value, arrived, total = push(source, row, level, columns, blocks[row], arrived, parts, after)
        (before if rising else turned_back)[level] = value
        if turn == LEV - 1:
            before[level] = value
        step = turn % (LEV - 1)
        parts, after = (), None
        if turn == 0:
            total = call(gram_kernel, sketch, [square], after=arrived[0])[0]
        if turn == LEV - 1:
            *ortho, total = call(ortho_kernel, [first, *sketch], [LEVEL_FIELD] * LEV + [square], after=arrived[0])
        if step < LEV - 2:
            parts = from_partners(total, steps[step])
        elif rising:
            first = after = call(functools.partial(factor_kernel, 1.0), [total], [square])[0]
        else:
            scale = math.sqrt(NB * BLOCK * count)
            second = call(functools.partial(factor_kernel, scale), [total], [square])[0]
    natural = [((S, NB * BLOCK), F32)]
    room = [pltpu.VMEM((S, NB * BLOCK), F32)]
    basis = call(basis_kernel, [plan, second, *ortho], natural, room)[0]
    both = jnp.dot(second, first, precision=HIGH)
    turned_back[0], _, _ = push(before[0], 0, 0, None, None, arrived, (), basis)
    adjoint_field = call(
        finish_kernel, [plan, both, inverse_blocks, *turned_back], natural, room
    )[0]
    return (basis, adjoint_field)


def solution(mesh):
    in_specs = (
        P(None, AXES),
        P(AXES, None),
        P(None, AXES),
        P(AXES, None),
        P(None, AXES),
        P(AXES, None),
        P(None, AXES),
        P(None, AXES),
        P(AXES, None),
    )
    out_specs = (P(None, AXES), P(None, AXES))
    return jax.shard_map(shards, mesh=mesh, in_specs=in_specs, out_specs=out_specs, check_vma=False)
```

```python
import functools
import math

import jax
import jax.numpy as jnp
from jax import lax
from jax.experimental import pallas as pl
from jax.experimental.pallas import tpu as pltpu
from jax.sharding import PartitionSpec as P

S = 32
BLOCK = 64
KL = 4
LEV = 8
RPL = 8
HB = 4
NB = 64
PAIR = 2 * BLOCK
QUAD = 4 * BLOCK
WIDE = RPL * BLOCK

HIGH = lax.Precision.HIGHEST
AXES = ("mesh", "grp")


def split(x):
    high = x.astype(jnp.bfloat16)
    low = (x - high.astype(jnp.float32)).astype(jnp.bfloat16)
    return high, low


def dot(a, b, dims=((1,), (0,))):
    return lax.dot_general(a, b, (dims, ((), ())), preferred_element_type=jnp.float32)


def dot3(a, b_high, b_low, dims=((1,), (0,))):
    a_high, a_low = split(a)
    return dot(a_high, b_high, dims) + (dot(a_low, b_high, dims) + dot(a_high, b_low, dims))


def first_half():
    return lax.broadcasted_iota(jnp.int32, (S, PAIR), 1) < BLOCK


def turned(tile):
    return pltpu.roll(tile, BLOCK, 1)


def doubled(tile):
    first = first_half()
    other = turned(tile)
    return jnp.where(first, tile, other), jnp.where(first, other, tile)


def parity_of(index):
    return jnp.bitwise_and(index, 1)


def pair_tile(ref, block):
    start = pl.multiple_of(lax.shift_right_logical(block, 1) * PAIR, PAIR)
    return pl.ds(start, PAIR)


def in_half(tile, block, half):
    return jnp.where(parity_of(block) == half, tile, turned(tile))


def listed(halo, level, ref):
    tiles = []
    first = first_half()
    for pair in range(HB // 2):
        h = [halo[2 * pair + half, level] for half in range(2)]
        moved = [in_half(ref[:, pair_tile(ref, h[half])], h[half], half) for half in range(2)]
        tiles.append(jnp.where(first, moved[0], moved[1]))
    return jnp.concatenate(tiles, axis=1)


def own_blocks(out):
    first = first_half()
    rows = [out[j * S : (j + 1) * S] for j in range(4)]
    return jnp.concatenate(
        [
            jnp.where(first, rows[0][:, :PAIR], rows[1][:, :PAIR]),
            jnp.where(first, rows[2][:, PAIR:], rows[3][:, PAIR:]),
        ],
        axis=1,
    )


def spread(quad):
    lane = lax.shift_right_logical(lax.broadcasted_iota(jnp.int32, (S, QUAD), 1), 6)
    return jnp.concatenate([jnp.where(lane == j, quad, 0.0) for j in range(4)], axis=0)


def stacked(quad):
    parts = []
    for pair in range(2):
        tile = quad[:, pair * PAIR : (pair + 1) * PAIR]
        parts += [tile[:, :BLOCK], turned(tile)[:, :BLOCK]]
    return jnp.concatenate(parts, axis=0)


def from_neighbour(swap1, spare):
    last = lax.axis_size("mesh") * lax.axis_size("grp") - 1
    place = lax.axis_index("mesh") * lax.axis_size("grp") + lax.axis_index("grp")
    end = jnp.logical_or(place == 0, place == last)
    beside = jnp.logical_or(place == 1, place == last - 1)
    return jnp.where(end, 0.0, jnp.where(beside, spare[...], swap1[...]))


def parity():
    return parity_of(lax.axis_index("grp"))


def prepare_kernel(level, plan, halo, forcing, inverse, out, *send):
    plan, halo = plan[...], halo[...]
    for quad in range(2):
        lanes = slice(quad * QUAD, (quad + 1) * QUAD)
        rows = []
        for j in range(4):
            block = plan[0, level * RPL + 4 * quad + j]
            tile = forcing[:, pair_tile(forcing, block)]
            rows.append(in_half(tile, block, 0)[:, :BLOCK])
        out[:, lanes] = own_blocks(dot3(jnp.concatenate(rows, axis=0), *split(inverse[:, lanes])))
    if send:
        send[0][...] = listed(halo, level, out)


def compose_kernel(blocks, inverse, high, low):
    lane = lax.shift_right_logical(lax.broadcasted_iota(jnp.int32, (BLOCK, QUAD), 1), 6)
    for quad in range(2):
        lanes = slice(quad * QUAD, (quad + 1) * QUAD)
        inv = inverse[:, lanes]
        diagonal = jnp.concatenate([jnp.where(lane == j, inv, 0.0) for j in range(4)], axis=0)
        d_high, d_low = split(diagonal)
        product = dot3(blocks[:, lanes], d_high, d_low)
        p_high, p_low = split(product)
        high[:, lanes] = p_high
        low[:, lanes] = p_low


def combine_kernel(level, halo, x, y, w, diag, inverse, out, *send):
    halo = halo[...]
    for quad in range(2):
        lanes = slice(quad * QUAD, (quad + 1) * QUAD)
        value = x[:, lanes]
        image = own_blocks(dot3(stacked(value), *split(diag[:, lanes])))
        image = own_blocks(dot3(stacked(image), *split(inverse[:, lanes])))
        out[:, lanes] = 2.0 * value + y[:, lanes] - w[:, lanes] - image
    if send:
        send[0][...] = listed(halo, level, out)


def fill_slots(slots, prev, swap0, swap1, spare):
    for pair in range(RPL // 2):
        a, b = doubled(prev[:, pair * PAIR : (pair + 1) * PAIR])
        slots[2 * pair] = a
        slots[2 * pair + 1] = b
    odd = parity()
    for ref, base in ((from_neighbour(swap1, spare), RPL + HB * odd), (swap0, RPL + HB - HB * odd)):
        for pair in range(HB // 2):
            a, b = doubled(ref[:, pair * PAIR : (pair + 1) * PAIR])
            slots[base + 2 * pair] = a
            slots[base + 2 * pair + 1] = b


def gather_kernel(row, level, columns, halo, base, high, low, prev, swap0, swap1, spare, out, *rest):
    columns, halo = columns[...], halo[...]
    slots = rest[-1]
    fill_slots(slots, prev, swap0, swap1, spare)
    first = first_half()
    for quad in range(2):
        rows = []
        for j in range(4):
            c = [columns[k, row * RPL + quad * 4 + j] for k in range(KL)]
            rows.append(
                jnp.concatenate(
                    [
                        jnp.where(first, slots[c[0]], slots[c[1]]),
                        jnp.where(first, slots[c[2]], slots[c[3]]),
                    ],
                    axis=1,
                )
            )
        lanes = slice(quad * QUAD, (quad + 1) * QUAD)
        product = dot3(jnp.concatenate(rows, axis=0), high[:, lanes], low[:, lanes])
        out[:, lanes] = base[:, lanes] - own_blocks(product)
    if len(rest) > 1:
        rest[0][...] = listed(halo, level, out)


def add_listed(halo, level, out, arriving):
    first = first_half()
    for i in range(HB):
        h = halo[i, level]
        tile = arriving[:, (i // 2) * PAIR : (i // 2 + 1) * PAIR]
        tile = jnp.where(parity_of(h) == i % 2, tile, turned(tile))
        keep = first == (parity_of(h) == 0)
        lanes = pair_tile(out, h)
        out[:, lanes] = out[:, lanes] - jnp.where(keep, tile, 0.0)


def push_kernel(row, level, parts, columns, halo, *refs):
    refs = list(refs)
    source = refs.pop(0)
    if halo is not None:
        halo = halo[...]
        own_in, swap0, swap1, spare = [refs.pop(0) for _ in range(4)]
    if columns is not None:
        columns = columns[...]
        high, low = refs.pop(0), refs.pop(0)
    if parts:
        total = refs.pop(0)[...]
        for _ in range(parts - 1):
            total = total + refs.pop(0)[...]
    if halo is not None:
        out = refs.pop(0)
        out[...] = source[...] - own_in[...]
        add_listed(halo, level, out, swap0[...] + from_neighbour(swap1, spare))
    else:
        out = source
    if columns is None:
        return
    own, send0, send1 = refs[:3]
    halves = refs[-1]
    if parts:
        refs[3][...] = total
    halves[...] = jnp.zeros_like(halves)
    first = first_half()
    for quad in range(2):
        lanes = slice(quad * QUAD, (quad + 1) * QUAD)
        terms = dot3(spread(out[:, lanes]), high[:, lanes], low[:, lanes], ((1,), (1,)))
        for j in range(4):
            for k in range(KL):
                c = columns[k, row * RPL + quad * 4 + j]
                tile = terms[j * S : (j + 1) * S, (k // 2) * PAIR : (k // 2 + 1) * PAIR]
                halves[k % 2, c] += tile

    def both_halves(c):
        value = jnp.where(first, halves[0, c], halves[1, c])
        return value + turned(value)

    for pair in range(RPL // 2):
        own[:, pair * PAIR : (pair + 1) * PAIR] = jnp.where(
            first, both_halves(2 * pair), both_halves(2 * pair + 1)
        )
    odd = parity()
    for ref, base in ((send1, RPL + HB * odd), (send0, RPL + HB - HB * odd)):
        for pair in range(HB // 2):
            ref[:, pair * PAIR : (pair + 1) * PAIR] = jnp.where(
                first, both_halves(base + 2 * pair), both_halves(base + 2 * pair + 1)
            )


def place(natural, block, piece, first):
    keep = first == (parity_of(block) == 0)
    lanes = pair_tile(natural, block)
    natural[:, lanes] = jnp.where(keep, piece, natural[:, lanes])


def full_dot(a, b, dims=((1,), (0,))):
    return lax.dot_general(a, b, (dims, ((), ())), precision=HIGH, preferred_element_type=jnp.float32)


def land(level, plan, field, inverse, out, turn=None):
    first = first_half()
    for quad in range(2):
        lanes = slice(quad * QUAD, (quad + 1) * QUAD)
        product = dot3(spread(field[:, lanes]), *split(inverse[:, lanes]), ((1,), (1,)))
        for j in range(4):
            piece = product[j * S : (j + 1) * S]
            if turn is not None:
                piece = full_dot(turn, piece)
            place(out, plan[0, level * RPL + 4 * quad + j], jnp.concatenate([piece, piece], axis=1), first)


def land_early_kernel(levels, plan, *refs):
    plan, out = plan[...], refs[-1]
    out[...] = jnp.zeros_like(out)
    for i, level in enumerate(levels):
        land(level, plan, refs[i], refs[len(levels) + i], out)


def land_mixed_kernel(level, plan, turn, start, field, inverse, out, natural):
    natural[...] = start[...]
    land(level, plan[...], field, inverse, natural)
    out[...] = full_dot(turn[...], natural[...])


def land_last_kernel(level, plan, turn, start, field, inverse, out):
    out[...] = start[...]
    land(level, plan[...], field, inverse, out, turn[...])


def basis_kernel(plan, turn, *refs):
    plan = plan[...]
    fields, out, natural = refs[:LEV], refs[LEV], refs[LEV + 1]
    first = first_half()
    for level in range(LEV):
        for pair in range(RPL // 2):
            a, b = doubled(fields[level][:, pair * PAIR : (pair + 1) * PAIR])
            at = level * RPL + 2 * pair
            place(natural, plan[0, at], a, first)
            place(natural, plan[0, at + 1], b, first)
    out[...] = full_dot(turn[...], natural[...])


def gram_kernel(fields, *refs):
    out = refs[-1]
    total = refs[fields][...] if len(refs) > fields + 1 else jnp.zeros((S, S), jnp.float32)
    for field in refs[:fields]:
        total = total + full_dot(field[...], field[...], ((1,), (1,)))
    out[...] = total


def factor_kernel(scale, gram, out):
    row = lax.broadcasted_iota(jnp.int32, (S, S), 0)
    unit = jnp.where(row == lax.broadcasted_iota(jnp.int32, (S, S), 1), 1.0, 0.0)
    table = jnp.concatenate([gram[...], unit], axis=1)
    below = lax.broadcasted_iota(jnp.int32, (S, 1), 0)
    pivots = jnp.ones((S, 1), jnp.float32)
    for k in range(S):
        pivot = table[k : k + 1, k : k + 1]
        pivots = jnp.where(below == k, pivot, pivots)
        factor = jnp.where(below > k, table[:, k : k + 1] / pivot, 0.0)
        table = table - factor * table[k : k + 1, :]
    out[...] = table[:, S:] * (scale / jnp.sqrt(pivots))


def ortho_kernel(turn, *refs):
    fields, outs, gram = refs[:LEV], refs[-LEV - 1 : -1], refs[-1]
    total = None
    for field, out in zip(fields, outs):
        value = full_dot(turn[...], field[...])
        out[...] = value
        part = full_dot(value, value, ((1,), (1,)))
        total = part if total is None else total + part
    gram[...] = total


VMEM_SPEC = pl.BlockSpec(memory_space=pltpu.VMEM)
ANY_SPEC = pl.BlockSpec(memory_space=pl.ANY)


def part(shape, place):
    return pl.BlockSpec(shape, lambda _: place)


def call(kernel, operands, outs, scratch=(), flops=0, after=None, vmem=6):
    name = getattr(kernel, "func", kernel).__name__
    pairs = [o if isinstance(o, tuple) else (o, VMEM_SPEC) for o in operands]
    if after is not None:
        inner, at = kernel, len(pairs)
        kernel = lambda *refs: inner(*refs[:at], *refs[at + 1 :])
        pairs.append((after, ANY_SPEC))
    moved = 4 * sum(math.prod(shape) for shape, _ in outs) * 2
    return pl.pallas_call(
        kernel,
        out_shape=[jax.ShapeDtypeStruct(shape, dtype) for shape, dtype in outs],
        grid=(1,) if any(spec.block_shape is not None for _, spec in pairs) else (),
        in_specs=[spec for _, spec in pairs],
        out_specs=[VMEM_SPEC] * len(outs),
        scratch_shapes=list(scratch),
        name=name,
        compiler_params=pltpu.CompilerParams(vmem_limit_bytes=vmem * 1024 * 1024),
        cost_estimate=pl.CostEstimate(flops=flops, bytes_accessed=moved, transcendentals=0),
    )(*[array for array, _ in pairs])


F32 = jnp.float32
BF16 = jnp.bfloat16
LEVEL_FIELD = ((S, WIDE), F32)
SENT = ((S, HB * BLOCK), F32)
SLOTS = pltpu.VMEM((RPL + 2 * HB, S, PAIR), F32)
HALVES = pltpu.VMEM((2, RPL + 2 * HB, S, PAIR), F32)


def swap(sent0, sent1):
    count = lax.axis_size(AXES)
    last = count - 1
    even = {i: i ^ 1 for i in range(count)}
    odd = {i: ((i + 1) ^ 1) - 1 for i in range(count)}
    odd.update({1: 2, 2: 0, 0: 1})
    odd.update({last - 1: last - 2, last - 2: last, last: last - 1})
    core = {i: i ^ 4 for i in range(count)}
    for start, end in ((2, 1), (last - 2, last - 1)):
        core.update({start: end, end: end ^ 4, end ^ 4: start ^ 4, start ^ 4: start})
    swap0 = lax.ppermute(sent0, AXES, sorted(even.items()))
    spare = lax.ppermute(sent1, AXES, sorted(core.items()))
    swap1 = lax.ppermute(sent1, AXES, sorted(odd.items()))
    return swap0, swap1, spare


def shards(forcing, plan, lower_blocks, lower_columns, upper_blocks, upper_columns, diag_blocks, inverse_blocks, halo_list):
    halo = halo_list.T
    lower_columns = lower_columns.T
    upper_columns = upper_columns.T
    square_at = lambda array, level: (array, part((BLOCK, WIDE), (0, level)))
    inverse = [square_at(inverse_blocks, level) for level in range(LEV)]
    diagonal = [square_at(diag_blocks, level) for level in range(LEV)]

    whole = lambda array: (array, part(array.shape, (0, 0)))

    def prepare(level, after=None):
        return call(
            functools.partial(prepare_kernel, level),
            [*((whole(plan), whole(halo), whole(forcing)) if level == 0 else (plan, halo, forcing)), inverse[level]],
            [LEVEL_FIELD, SENT] if level == 0 else [LEVEL_FIELD],
            after=after,
        )

    def compose(blocks, level, row):
        wide = ((KL * BLOCK, WIDE), BF16)
        tall = (blocks, part((KL * BLOCK, WIDE), (0, level)))
        return call(compose_kernel, [tall, inverse[row]], [wide, wide], flops=2 * 6 * 256**3)

    y0, sent = prepare(0)
    y = [y0] + [prepare(level, sent)[0] for level in range(1, LEV)]
    lower = [compose(lower_blocks, level, level + 1) for level in range(LEV - 1)]
    upper = [compose(upper_blocks, level, level) for level in range(LEV - 1)]

    def gather(base, blocks, columns, row, level, prev, sent, send_on):
        swaps = swap(sent, sent)
        outs = call(
            functools.partial(gather_kernel, row, level),
            [columns, halo, base, *blocks, prev, *swaps],
            [LEVEL_FIELD, SENT] if send_on else [LEVEL_FIELD],
            [SLOTS],
        )
        return (outs[0], outs[1]) if send_on else (outs[0], None)

    def ascend(base, sent):
        field = [base[0]]
        for level in range(1, LEV):
            value, sent = gather(
                base[level], lower[level - 1], lower_columns, level - 1, level, field[-1], sent, True
            )
            field.append(value)
        return field, sent

    def descend(base, sent):
        field = [None] * LEV
        field[LEV - 1] = base[LEV - 1]
        for level in range(LEV - 2, -1, -1):
            field[level], sent = gather(
                base[level], upper[level], upper_columns, level, level, field[level + 1], sent, level > 0
            )
        return field

    w, sent = ascend(y, sent)
    x = descend(w, sent)

    def combine(level):
        return call(
            functools.partial(combine_kernel, level),
            [halo, x[level], y[level], w[level], diagonal[level], inverse[level]],
            [LEVEL_FIELD, SENT] if level == 0 else [LEVEL_FIELD],
        )

    c0, sent = combine(0)
    c = [c0] + [combine(level)[0] for level in range(1, LEV)]
    v, sent = ascend(c, sent)
    sketch = descend([v[level] + w[level] - x[level] for level in range(LEV)], sent)

    count = lax.axis_size(AXES)
    square = ((S, S), F32)

    def push(source, row, level, columns, blocks, arrived, parts=(), after=None):
        kernel = functools.partial(push_kernel, row, level, len(parts))
        operands = [source]
        if arrived is None:
            kernel = functools.partial(push_kernel, row, level, len(parts))
            bound = lambda columns, *refs: kernel(columns, None, *refs)
            operands = [columns, *operands, *blocks, *parts]
            outs = []
        elif columns is None:
            bound = lambda halo, *refs: kernel(None, halo, *refs)
            operands = [halo, *operands, *arrived, *parts]
            outs = [LEVEL_FIELD]
        else:
            bound = lambda columns, halo, *refs: kernel(columns, halo, *refs)
            operands = [columns, halo, *operands, *arrived, *blocks, *parts]
            outs = [LEVEL_FIELD]
        bound.__name__ = "push_kernel"
        if columns is not None:
            outs = outs + [LEVEL_FIELD, SENT, SENT] + ([square] if parts else [])
        results = list(call(bound, operands, outs, [HALVES] if columns is not None else [], after=after))
        value = source if arrived is None else results.pop(0)
        if columns is None:
            return value, None, None
        total = results.pop(3) if parts else None
        return value, (results[0], *swap(results[1], results[2])), total

    def from_partners(part, distances):
        return [part] + [lax.ppermute(part, AXES, [(i, i ^ far) for i in range(count)]) for far in distances]

    steps = [(4, 8, 12), (1,), (2,), (16,), (32,), (64,)]
    levels = [(level, level, upper_columns, upper) for level in range(LEV - 1)]
    levels += [(level, level - 1, lower_columns, lower) for level in range(LEV - 1, 0, -1)]
    natural = [((S, NB * BLOCK), F32)]
    room = [pltpu.VMEM((S, NB * BLOCK), F32)]
    before = [None] * LEV
    turned_back = [None] * LEV
    arrived = None
    local = call(functools.partial(gram_kernel, LEV - 1), sketch[1:], [square])[0]
    after = local = call(functools.partial(gram_kernel, 1), [sketch[0], local], [square])[0]
    parts = ()
    for turn, (level, row, columns, blocks) in enumerate(levels):
        rising = turn < LEV - 1
        source = sketch[level] if turn < LEV else before[level]
        value, arrived, total = push(source, row, level, columns, blocks[row], arrived, parts, after)
        (before if rising else turned_back)[level] = value
        if turn == LEV - 1:
            before[level] = value
        step = turn % (LEV - 1)
        local, parts, after = after, (), None
        if turn in (0, LEV - 1):
            total = local
        if turn == len(levels) - 2:
            early = list(range(2, LEV))
            landed = after = call(
                functools.partial(land_early_kernel, early),
                [plan, *[turned_back[k] for k in early], *[inverse[k] for k in early]],
                natural,
                after=arrived[0],
            )[0]
        if step < LEV - 2:
            parts = from_partners(total, steps[step])
        elif rising:
            first = call(functools.partial(factor_kernel, 1.0), [total], [square])[0]
            *ortho, after = call(ortho_kernel, [first, *sketch], [LEVEL_FIELD] * LEV + [square])
        else:
            scale = math.sqrt(NB * BLOCK * count)
            second = call(functools.partial(factor_kernel, scale), [total], [square])[0]
    basis = call(basis_kernel, [plan, second, *ortho], natural, room)[0]
    both = jnp.dot(second, first, precision=HIGH)
    landed = call(
        functools.partial(land_mixed_kernel, 1),
        [plan, both, landed, turned_back[1], inverse[1]],
        natural,
        room,
        after=basis,
    )[0]
    turned_back[0], _, _ = push(before[0], 0, 0, None, None, arrived, (), landed)
    adjoint_field = call(
        functools.partial(land_last_kernel, 0), [plan, both, landed, turned_back[0], inverse[0]], natural
    )[0]
    return (basis, adjoint_field)


def solution(mesh):
    in_specs = (
        P(None, AXES),
        P(AXES, None),
        P(None, AXES),
        P(AXES, None),
        P(None, AXES),
        P(AXES, None),
        P(None, AXES),
        P(None, AXES),
        P(AXES, None),
    )
    out_specs = (P(None, AXES), P(None, AXES))
    return jax.shard_map(shards, mesh=mesh, in_specs=in_specs, out_specs=out_specs, check_vma=False)
```

```python
import functools
import math

import jax
import jax.numpy as jnp
from jax import lax
from jax.experimental import pallas as pl
from jax.experimental.pallas import tpu as pltpu
from jax.sharding import PartitionSpec as P

S = 32
BLOCK = 64
KL = 4
LEV = 8
RPL = 8
HB = 4
NB = 64
PAIR = 2 * BLOCK
QUAD = 4 * BLOCK
WIDE = RPL * BLOCK

HIGH = lax.Precision.HIGHEST
AXES = ("mesh", "grp")


def split(x):
    high = x.astype(jnp.bfloat16)
    low = (x - high.astype(jnp.float32)).astype(jnp.bfloat16)
    return high, low


def dot(a, b, dims=((1,), (0,))):
    return lax.dot_general(a, b, (dims, ((), ())), preferred_element_type=jnp.float32)


def dot3(a, b_high, b_low, dims=((1,), (0,))):
    a_high, a_low = split(a)
    return dot(a_high, b_high, dims) + (dot(a_low, b_high, dims) + dot(a_high, b_low, dims))


def first_half():
    return lax.broadcasted_iota(jnp.int32, (S, PAIR), 1) < BLOCK


def turned(tile):
    return pltpu.roll(tile, BLOCK, 1)


def doubled(tile):
    first = first_half()
    other = turned(tile)
    return jnp.where(first, tile, other), jnp.where(first, other, tile)


def parity_of(index):
    return jnp.bitwise_and(index, 1)


def pair_tile(ref, block):
    start = pl.multiple_of(lax.shift_right_logical(block, 1) * PAIR, PAIR)
    return pl.ds(start, PAIR)


def in_half(tile, block, half):
    return jnp.where(parity_of(block) == half, tile, turned(tile))


def listed(halo, level, ref):
    tiles = []
    first = first_half()
    for pair in range(HB // 2):
        h = [halo[2 * pair + half, level] for half in range(2)]
        moved = [in_half(ref[:, pair_tile(ref, h[half])], h[half], half) for half in range(2)]
        tiles.append(jnp.where(first, moved[0], moved[1]))
    return jnp.concatenate(tiles, axis=1)


def own_blocks(out):
    first = first_half()
    rows = [out[j * S : (j + 1) * S] for j in range(4)]
    return jnp.concatenate(
        [
            jnp.where(first, rows[0][:, :PAIR], rows[1][:, :PAIR]),
            jnp.where(first, rows[2][:, PAIR:], rows[3][:, PAIR:]),
        ],
        axis=1,
    )


def spread(quad):
    lane = lax.shift_right_logical(lax.broadcasted_iota(jnp.int32, (S, QUAD), 1), 6)
    return jnp.concatenate([jnp.where(lane == j, quad, 0.0) for j in range(4)], axis=0)


def stacked(quad):
    parts = []
    for pair in range(2):
        tile = quad[:, pair * PAIR : (pair + 1) * PAIR]
        parts += [tile[:, :BLOCK], turned(tile)[:, :BLOCK]]
    return jnp.concatenate(parts, axis=0)


def from_neighbour(swap1, spare):
    last = lax.axis_size("mesh") * lax.axis_size("grp") - 1
    place = lax.axis_index("mesh") * lax.axis_size("grp") + lax.axis_index("grp")
    end = jnp.logical_or(place == 0, place == last)
    beside = jnp.logical_or(place == 1, place == last - 1)
    return jnp.where(end, 0.0, jnp.where(beside, spare[...], swap1[...]))


def parity():
    return parity_of(lax.axis_index("grp"))


def prepare_kernel(level, plan, halo, forcing, inverse, out, *send):
    plan, halo = plan[...], halo[...]
    for quad in range(2):
        lanes = slice(quad * QUAD, (quad + 1) * QUAD)
        rows = []
        for j in range(4):
            block = plan[0, level * RPL + 4 * quad + j]
            tile = forcing[:, pair_tile(forcing, block)]
            rows.append(in_half(tile, block, 0)[:, :BLOCK])
        out[:, lanes] = own_blocks(dot3(jnp.concatenate(rows, axis=0), *split(inverse[:, lanes])))
    if send:
        send[0][...] = listed(halo, level, out)


def compose_kernel(blocks, inverse, high, low):
    lane = lax.shift_right_logical(lax.broadcasted_iota(jnp.int32, (BLOCK, QUAD), 1), 6)
    for quad in range(2):
        lanes = slice(quad * QUAD, (quad + 1) * QUAD)
        inv = inverse[:, lanes]
        diagonal = jnp.concatenate([jnp.where(lane == j, inv, 0.0) for j in range(4)], axis=0)
        d_high, d_low = split(diagonal)
        product = dot3(blocks[:, lanes], d_high, d_low)
        p_high, p_low = split(product)
        high[:, lanes] = p_high
        low[:, lanes] = p_low


def combine_kernel(level, halo, x, y, w, diag, inverse, out, *send):
    halo = halo[...]
    for quad in range(2):
        lanes = slice(quad * QUAD, (quad + 1) * QUAD)
        value = x[:, lanes]
        image = own_blocks(dot3(stacked(value), *split(diag[:, lanes])))
        image = own_blocks(dot3(stacked(image), *split(inverse[:, lanes])))
        out[:, lanes] = 2.0 * value + y[:, lanes] - w[:, lanes] - image
    if send:
        send[0][...] = listed(halo, level, out)


def fill_slots(slots, prev, swap0, swap1, spare):
    for pair in range(RPL // 2):
        a, b = doubled(prev[:, pair * PAIR : (pair + 1) * PAIR])
        slots[2 * pair] = a
        slots[2 * pair + 1] = b
    odd = parity()
    for ref, base in ((from_neighbour(swap1, spare), RPL + HB * odd), (swap0, RPL + HB - HB * odd)):
        for pair in range(HB // 2):
            a, b = doubled(ref[:, pair * PAIR : (pair + 1) * PAIR])
            slots[base + 2 * pair] = a
            slots[base + 2 * pair + 1] = b


def gather_kernel(row, level, columns, halo, base, high, low, prev, swap0, swap1, spare, out, *rest):
    columns, halo = columns[...], halo[...]
    slots = rest[-1]
    fill_slots(slots, prev, swap0, swap1, spare)
    first = first_half()
    for quad in range(2):
        rows = []
        for j in range(4):
            c = [columns[k, row * RPL + quad * 4 + j] for k in range(KL)]
            rows.append(
                jnp.concatenate(
                    [
                        jnp.where(first, slots[c[0]], slots[c[1]]),
                        jnp.where(first, slots[c[2]], slots[c[3]]),
                    ],
                    axis=1,
                )
            )
        lanes = slice(quad * QUAD, (quad + 1) * QUAD)
        product = dot3(jnp.concatenate(rows, axis=0), high[:, lanes], low[:, lanes])
        out[:, lanes] = base[:, lanes] - own_blocks(product)
    if len(rest) > 1:
        rest[0][...] = listed(halo, level, out)


def add_listed(halo, level, out, arriving):
    first = first_half()
    for i in range(HB):
        h = halo[i, level]
        tile = arriving[:, (i // 2) * PAIR : (i // 2 + 1) * PAIR]
        tile = jnp.where(parity_of(h) == i % 2, tile, turned(tile))
        keep = first == (parity_of(h) == 0)
        lanes = pair_tile(out, h)
        out[:, lanes] = out[:, lanes] - jnp.where(keep, tile, 0.0)


def push_kernel(row, level, parts, columns, halo, *refs):
    refs = list(refs)
    source = refs.pop(0)
    if halo is not None:
        halo = halo[...]
        own_in, swap0, swap1, spare = [refs.pop(0) for _ in range(4)]
    if columns is not None:
        columns = columns[...]
        high, low = refs.pop(0), refs.pop(0)
    if parts:
        total = refs.pop(0)[...]
        for _ in range(parts - 1):
            total = total + refs.pop(0)[...]
    if halo is not None:
        out = refs.pop(0)
        out[...] = source[...] - own_in[...]
        add_listed(halo, level, out, swap0[...] + from_neighbour(swap1, spare))
    else:
        out = source
    if columns is None:
        return
    own, send0, send1 = refs[:3]
    halves = refs[-2:]
    if parts:
        refs[3][...] = total
    for half in halves:
        half[...] = jnp.zeros_like(half)
    first = first_half()
    for quad in range(2):
        lanes = slice(quad * QUAD, (quad + 1) * QUAD)
        terms = dot3(spread(out[:, lanes]), high[:, lanes], low[:, lanes], ((1,), (1,)))
        for j in range(4):
            for k in range(KL):
                c = columns[k, row * RPL + quad * 4 + j]
                tile = terms[j * S : (j + 1) * S, (k // 2) * PAIR : (k // 2 + 1) * PAIR]
                halves[k % 2][c] += tile

    def both_halves(c):
        value = jnp.where(first, halves[0][c], halves[1][c])
        return value + turned(value)

    for pair in range(RPL // 2):
        own[:, pair * PAIR : (pair + 1) * PAIR] = jnp.where(
            first, both_halves(2 * pair), both_halves(2 * pair + 1)
        )
    odd = parity()
    for ref, base in ((send1, RPL + HB * odd), (send0, RPL + HB - HB * odd)):
        for pair in range(HB // 2):
            ref[:, pair * PAIR : (pair + 1) * PAIR] = jnp.where(
                first, both_halves(base + 2 * pair), both_halves(base + 2 * pair + 1)
            )


def place(natural, block, piece, first):
    keep = first == (parity_of(block) == 0)
    lanes = pair_tile(natural, block)
    natural[:, lanes] = jnp.where(keep, piece, natural[:, lanes])


def full_dot(a, b, dims=((1,), (0,))):
    return lax.dot_general(a, b, (dims, ((), ())), precision=HIGH, preferred_element_type=jnp.float32)


def land(level, plan, field, inverse, out, turn=None):
    first = first_half()
    for quad in range(2):
        lanes = slice(quad * QUAD, (quad + 1) * QUAD)
        product = dot3(spread(field[:, lanes]), *split(inverse[:, lanes]), ((1,), (1,)))
        for j in range(4):
            piece = product[j * S : (j + 1) * S]
            if turn is not None:
                piece = full_dot(turn, piece)
            place(out, plan[0, level * RPL + 4 * quad + j], jnp.concatenate([piece, piece], axis=1), first)


def land_early_kernel(levels, plan, *refs):
    plan, out = plan[...], refs[-1]
    out[...] = jnp.zeros_like(out)
    for i, level in enumerate(levels):
        land(level, plan, refs[i], refs[len(levels) + i], out)


def land_mixed_kernel(level, plan, turn, start, field, inverse, out, natural):
    natural[...] = start[...]
    land(level, plan[...], field, inverse, natural)
    out[...] = full_dot(turn[...], natural[...])


def land_last_kernel(level, plan, turn, start, field, inverse, out):
    out[...] = start[...]
    land(level, plan[...], field, inverse, out, turn[...])


def basis_kernel(plan, turn, *refs):
    plan = plan[...]
    fields, out, natural = refs[:LEV], refs[LEV], refs[LEV + 1]
    first = first_half()
    for level in range(LEV):
        for pair in range(RPL // 2):
            a, b = doubled(fields[level][:, pair * PAIR : (pair + 1) * PAIR])
            at = level * RPL + 2 * pair
            place(natural, plan[0, at], a, first)
            place(natural, plan[0, at + 1], b, first)
    out[...] = full_dot(turn[...], natural[...])


def gram_kernel(fields, *refs):
    out = refs[-1]
    total = refs[fields][...] if len(refs) > fields + 1 else jnp.zeros((S, S), jnp.float32)
    for field in refs[:fields]:
        total = total + full_dot(field[...], field[...], ((1,), (1,)))
    out[...] = total


def factor_kernel(scale, gram, out):
    row = lax.broadcasted_iota(jnp.int32, (S, S), 0)
    unit = jnp.where(row == lax.broadcasted_iota(jnp.int32, (S, S), 1), 1.0, 0.0)
    table = jnp.concatenate([gram[...], unit], axis=1)
    below = lax.broadcasted_iota(jnp.int32, (S, 1), 0)
    pivots = jnp.ones((S, 1), jnp.float32)
    for k in range(S):
        pivot = table[k : k + 1, k : k + 1]
        pivots = jnp.where(below == k, pivot, pivots)
        factor = jnp.where(below > k, table[:, k : k + 1] / pivot, 0.0)
        table = table - factor * table[k : k + 1, :]
    out[...] = table[:, S:] * (scale / jnp.sqrt(pivots))


def ortho_kernel(turn, *refs):
    fields, outs, gram = refs[:LEV], refs[-LEV - 1 : -1], refs[-1]
    total = None
    for field, out in zip(fields, outs):
        value = full_dot(turn[...], field[...])
        out[...] = value
        part = full_dot(value, value, ((1,), (1,)))
        total = part if total is None else total + part
    gram[...] = total


VMEM_SPEC = pl.BlockSpec(memory_space=pltpu.VMEM)
ANY_SPEC = pl.BlockSpec(memory_space=pl.ANY)


def part(shape, place):
    return pl.BlockSpec(shape, lambda _: place)


def call(kernel, operands, outs, scratch=(), flops=0, after=None, vmem=6):
    name = getattr(kernel, "func", kernel).__name__
    pairs = [o if isinstance(o, tuple) else (o, VMEM_SPEC) for o in operands]
    if after is not None:
        inner, at = kernel, len(pairs)
        kernel = lambda *refs: inner(*refs[:at], *refs[at + 1 :])
        pairs.append((after, ANY_SPEC))
    moved = 4 * sum(math.prod(shape) for shape, _ in outs) * 2
    return pl.pallas_call(
        kernel,
        out_shape=[jax.ShapeDtypeStruct(shape, dtype) for shape, dtype in outs],
        grid=(1,) if any(spec.block_shape is not None for _, spec in pairs) else (),
        in_specs=[spec for _, spec in pairs],
        out_specs=[VMEM_SPEC] * len(outs),
        scratch_shapes=list(scratch),
        name=name,
        compiler_params=pltpu.CompilerParams(vmem_limit_bytes=vmem * 1024 * 1024),
        cost_estimate=pl.CostEstimate(flops=flops, bytes_accessed=moved, transcendentals=0),
    )(*[array for array, _ in pairs])


F32 = jnp.float32
BF16 = jnp.bfloat16
LEVEL_FIELD = ((S, WIDE), F32)
SENT = ((S, HB * BLOCK), F32)
SLOTS = pltpu.VMEM((RPL + 2 * HB, S, PAIR), F32)


def swap(sent0, sent1):
    count = lax.axis_size(AXES)
    last = count - 1
    even = {i: i ^ 1 for i in range(count)}
    odd = {i: ((i + 1) ^ 1) - 1 for i in range(count)}
    odd.update({1: 2, 2: 0, 0: 1})
    odd.update({last - 1: last - 2, last - 2: last, last: last - 1})
    core = {i: i ^ 4 for i in range(count)}
    for start, end in ((2, 1), (last - 2, last - 1)):
        core.update({start: end, end: end ^ 4, end ^ 4: start ^ 4, start ^ 4: start})
    swap0 = lax.ppermute(sent0, AXES, sorted(even.items()))
    spare = lax.ppermute(sent1, AXES, sorted(core.items()))
    swap1 = lax.ppermute(sent1, AXES, sorted(odd.items()))
    return swap0, swap1, spare


def shards(forcing, plan, lower_blocks, lower_columns, upper_blocks, upper_columns, diag_blocks, inverse_blocks, halo_list):
    halo = halo_list.T
    lower_columns = lower_columns.T
    upper_columns = upper_columns.T
    square_at = lambda array, level: (array, part((BLOCK, WIDE), (0, level)))
    inverse = [square_at(inverse_blocks, level) for level in range(LEV)]
    diagonal = [square_at(diag_blocks, level) for level in range(LEV)]

    whole = lambda array: (array, part(array.shape, (0, 0)))

    def prepare(level, after=None):
        return call(
            functools.partial(prepare_kernel, level),
            [*((whole(plan), whole(halo), whole(forcing)) if level == 0 else (plan, halo, forcing)), inverse[level]],
            [LEVEL_FIELD, SENT] if level == 0 else [LEVEL_FIELD],
            after=after,
        )

    def compose(blocks, level, row):
        wide = ((KL * BLOCK, WIDE), BF16)
        tall = (blocks, part((KL * BLOCK, WIDE), (0, level)))
        return call(compose_kernel, [tall, inverse[row]], [wide, wide], flops=2 * 6 * 256**3)

    y0, sent = prepare(0)
    y = [y0] + [prepare(level, sent)[0] for level in range(1, LEV)]
    lower = [compose(lower_blocks, level, level + 1) for level in range(LEV - 1)]
    upper = [compose(upper_blocks, level, level) for level in range(LEV - 1)]

    def gather(base, blocks, columns, row, level, prev, sent, send_on):
        swaps = swap(sent, sent)
        outs = call(
            functools.partial(gather_kernel, row, level),
            [columns, halo, base, *blocks, prev, *swaps],
            [LEVEL_FIELD, SENT] if send_on else [LEVEL_FIELD],
            [SLOTS],
        )
        return (outs[0], outs[1]) if send_on else (outs[0], None)

    def ascend(base, sent):
        field = [base[0]]
        for level in range(1, LEV):
            value, sent = gather(
                base[level], lower[level - 1], lower_columns, level - 1, level, field[-1], sent, True
            )
            field.append(value)
        return field, sent

    def descend(base, sent):
        field = [None] * LEV
        field[LEV - 1] = base[LEV - 1]
        for level in range(LEV - 2, -1, -1):
            field[level], sent = gather(
                base[level], upper[level], upper_columns, level, level, field[level + 1], sent, level > 0
            )
        return field

    w, sent = ascend(y, sent)
    x = descend(w, sent)

    def combine(level):
        return call(
            functools.partial(combine_kernel, level),
            [halo, x[level], y[level], w[level], diagonal[level], inverse[level]],
            [LEVEL_FIELD, SENT] if level == 0 else [LEVEL_FIELD],
        )

    c0, sent = combine(0)
    c = [c0] + [combine(level)[0] for level in range(1, LEV)]
    v, sent = ascend(c, sent)
    sketch = descend([v[level] + w[level] - x[level] for level in range(LEV)], sent)

    count = lax.axis_size(AXES)
    square = ((S, S), F32)

    def push(source, row, level, columns, blocks, arrived, parts=(), after=None):
        kernel = functools.partial(push_kernel, row, level, len(parts))
        operands = [source]
        if arrived is None:
            kernel = functools.partial(push_kernel, row, level, len(parts))
            bound = lambda columns, *refs: kernel(columns, None, *refs)
            operands = [columns, *operands, *blocks, *parts]
            outs = []
        elif columns is None:
            bound = lambda halo, *refs: kernel(None, halo, *refs)
            operands = [halo, *operands, *arrived, *parts]
            outs = [LEVEL_FIELD]
        else:
            bound = lambda columns, halo, *refs: kernel(columns, halo, *refs)
            operands = [columns, halo, *operands, *arrived, *blocks, *parts]
            outs = [LEVEL_FIELD]
        bound.__name__ = "push_kernel"
        if columns is not None:
            outs = outs + [LEVEL_FIELD, SENT, SENT] + ([square] if parts else [])
        results = list(call(bound, operands, outs, [SLOTS, SLOTS] if columns is not None else [], after=after))
        value = source if arrived is None else results.pop(0)
        if columns is None:
            return value, None, None
        total = results.pop(3) if parts else None
        return value, (results[0], *swap(results[1], results[2])), total

    def from_partners(part, distances):
        return [part] + [lax.ppermute(part, AXES, [(i, i ^ far) for i in range(count)]) for far in distances]

    steps = [(4, 8, 12), (1,), (2,), (16,), (32,), (64,)]
    levels = [(level, level, upper_columns, upper) for level in range(LEV - 1)]
    levels += [(level, level - 1, lower_columns, lower) for level in range(LEV - 1, 0, -1)]
    natural = [((S, NB * BLOCK), F32)]
    room = [pltpu.VMEM((S, NB * BLOCK), F32)]
    before = [None] * LEV
    turned_back = [None] * LEV
    arrived = None
    local = call(functools.partial(gram_kernel, LEV - 1), sketch[1:], [square])[0]
    after = local = call(functools.partial(gram_kernel, 1), [sketch[0], local], [square])[0]
    parts = ()
    for turn, (level, row, columns, blocks) in enumerate(levels):
        rising = turn < LEV - 1
        source = sketch[level] if turn < LEV else before[level]
        value, arrived, total = push(source, row, level, columns, blocks[row], arrived, parts, after)
        (before if rising else turned_back)[level] = value
        if turn == LEV - 1:
            before[level] = value
        step = turn % (LEV - 1)
        local, parts, after = after, (), None
        if turn in (0, LEV - 1):
            total = local
        if turn == len(levels) - 2:
            early = list(range(2, LEV))
            landed = after = call(
                functools.partial(land_early_kernel, early),
                [plan, *[turned_back[k] for k in early], *[inverse[k] for k in early]],
                natural,
                after=arrived[0],
            )[0]
        if step < LEV - 2:
            parts = from_partners(total, steps[step])
        elif rising:
            first = call(functools.partial(factor_kernel, 1.0), [total], [square])[0]
            *ortho, after = call(ortho_kernel, [first, *sketch], [LEVEL_FIELD] * LEV + [square])
        else:
            scale = math.sqrt(NB * BLOCK * count)
            second = call(functools.partial(factor_kernel, scale), [total], [square])[0]
    basis = call(basis_kernel, [plan, second, *ortho], natural, room)[0]
    both = jnp.dot(second, first, precision=HIGH)
    landed = call(
        functools.partial(land_mixed_kernel, 1),
        [plan, both, landed, turned_back[1], inverse[1]],
        natural,
        room,
        after=basis,
    )[0]
    turned_back[0], _, _ = push(before[0], 0, 0, None, None, arrived, (), landed)
    adjoint_field = call(
        functools.partial(land_last_kernel, 0), [plan, both, landed, turned_back[0], inverse[0]], natural
    )[0]
    return (basis, adjoint_field)


def solution(mesh):
    in_specs = (
        P(None, AXES),
        P(AXES, None),
        P(None, AXES),
        P(AXES, None),
        P(None, AXES),
        P(AXES, None),
        P(None, AXES),
        P(None, AXES),
        P(AXES, None),
    )
    out_specs = (P(None, AXES), P(None, AXES))
    return jax.shard_map(shards, mesh=mesh, in_specs=in_specs, out_specs=out_specs, check_vma=False)
```
